32 devices in a mesh: dp: 16 (over z, y, x), tensor: 2 (over core).
Axes of the slice: x: 2, y: 2, z: 4, core: 2. Of those that a mesh axis runs over, the one named last changes fastest.
Arguments:
- activations: bfloat16 [4096, 53248], P('dp', 'tensor'), may hold values from -32 to 32
- test_matrix: bfloat16 [53248, 256], P('tensor', 'dp'), may hold values from -0.02734375 to 0.02734375
- gradient: bfloat16 [53248, 8192], P('tensor', 'dp'), may hold values from -16 to 16
Outputs:
- preconditioned: bfloat16 [53248, 8192], P('tensor', 'dp')
- gram_matrix: float32 [256, 256], replicated
The draws below stay inside these ranges and needn't reach their ends.
All inputs are finite; a program needn't handle non-finite values.
Results may differ from the reference program's by a relative error of at most 0.0034.
Values may be sent and summed in bfloat16 or wider, within the bound.
No kernel may reach another device: no remote copies, remote signals or barrier semaphores. Data moves between devices by JAX's collectives and lax.ppermute only.
A program may use at most 192 MiB of HBM per device.

```python
import math
import jax
import jax.numpy as jnp
from jax import lax

INNER_WIDTH = 53248
GRAD_COLS = 8192
SKETCH_RANK = 256
TOKENS = 4096


def feature_scales(key):
    scale_key = jax.random.fold_in(key, 9173)
    return jnp.exp(jax.random.uniform(scale_key, (INNER_WIDTH,), jnp.float32, 0.0, math.log(10.0)))


def draw_activations(key, part):
    scales = feature_scales(key)
    base_key = jax.random.fold_in(key, 11)
    row_key = jax.random.fold_in(key, 12)
    position = jnp.arange(TOKENS, dtype=jnp.float32) / max(TOKENS - 1, 1)
    row_scale = jnp.exp(position * math.log(3.0) + jax.random.uniform(row_key, (TOKENS,), jnp.float32, 0.0, math.log(3.0)))
    values = jax.random.normal(base_key, (TOKENS, INNER_WIDTH), jnp.float32)
    values = values * row_scale[:, None] * scales[None, :] / 8.0
    return jnp.clip(values, -32.0, 32.0).astype(jnp.bfloat16)


def draw_gradient(key, part):
    scales = feature_scales(key)
    base_key = jax.random.fold_in(key, 21)
    values = jax.random.normal(base_key, (INNER_WIDTH, GRAD_COLS), jnp.float32)
    values = values * scales[:, None] / 2.0
    return jnp.clip(values, -16.0, 16.0).astype(jnp.bfloat16)


def block_scale(own_key, extent, cuts, least, top_value):
    def one(dim, blocks):
        draws = jax.random.uniform(jax.random.fold_in(jax.random.fold_in(own_key, 6), dim), (blocks,), jnp.float32, least / len(cuts), top_value / len(cuts))
        return jnp.repeat(jnp.exp(draws), extent[dim] // blocks).reshape((-1,) + (1,) * (len(extent) - dim - 1))

    level = one(*cuts[0])
    for cut in cuts[1:]:
        level = level * one(*cut)
    return level


def gaussian(key, shape, scale, limit, shards=(), kind=jnp.bfloat16):
    entries = jax.random.normal(key, shape, jnp.float32) * scale
    if len(shards) > 0:
        entries = block_scale(key, shape, shards, -0.22, 0.18) * entries
    return jnp.clip(entries, min=-limit, max=limit).astype(kind)


def setup_inputs(seed: int = 0) -> dict:
    arg_keys = jax.random.split(jax.random.key(seed), 4)
    return {
        "activations": draw_activations(jax.random.fold_in(arg_keys[3], 71), 0),
        "test_matrix": gaussian(arg_keys[1], (INNER_WIDTH, SKETCH_RANK), INNER_WIDTH ** -0.5, 0.02734375, ((0, 2), (1, 16))),
        "gradient": draw_gradient(jax.random.fold_in(arg_keys[3], 71), 0),
    }


damping_ratio = 0.1

def symmetric(matrix):
    return 0.5 * (matrix + matrix.T)

def reference(activations, test_matrix, gradient):
    tokens = activations.shape[0]
    sketch = jnp.dot(activations.astype(jnp.float32), test_matrix.astype(jnp.float32), preferred_element_type=jnp.float32)
    sketch_low = sketch.astype(jnp.bfloat16)
    factor = lax.dot_general(activations.astype(jnp.float32), sketch_low.astype(jnp.float32), (((0,), (0,)), ((), ())), preferred_element_type=jnp.float32) / tokens
    core_matrix = symmetric(jnp.dot(test_matrix.astype(jnp.float32).T, factor, precision=lax.Precision.HIGHEST))
    chol_lower = jnp.linalg.cholesky(core_matrix)
    basis_full = jax.scipy.linalg.solve_triangular(chol_lower, factor.T, lower=True).T
    gram_matrix = jnp.dot(basis_full.T, basis_full, precision=lax.Precision.HIGHEST)
    damping = damping_ratio * jnp.trace(gram_matrix) / SKETCH_RANK
    kernel_lower = jnp.linalg.cholesky(gram_matrix + damping * jnp.eye(SKETCH_RANK, dtype=jnp.float32))
    basis_low = basis_full.astype(jnp.bfloat16)
    projected = lax.dot_general(basis_low.astype(jnp.float32), gradient.astype(jnp.float32), (((0,), (0,)), ((), ())), preferred_element_type=jnp.float32)
    weights = jax.scipy.linalg.cho_solve((kernel_lower, True), projected).astype(jnp.bfloat16)
    correction = jnp.dot(basis_low.astype(jnp.float32), weights.astype(jnp.float32), preferred_element_type=jnp.float32)
    return ((gradient.astype(jnp.float32) - correction).astype(jnp.bfloat16), gram_matrix)
```

```python
import jax
import jax.numpy as jnp
from jax import lax
from jax.experimental import pallas as pl
from jax.experimental.pallas import tpu as pltpu
from jax.sharding import PartitionSpec as P

damping_ratio = 0.1
exact = lax.Precision.HIGHEST
megabyte = 1024 * 1024


def mul(a, b, dims=((1,), (0,))):
    return lax.dot_general(a, b, (dims, ((), ())), precision=exact, preferred_element_type=jnp.float32)


def low_mul(a, b, dims=((1,), (0,))):
    return lax.dot_general(a, b, (dims, ((), ())), preferred_element_type=jnp.float32)


def across(value, bit):
    count = lax.axis_size("dp")
    return lax.ppermute(value, "dp", [(i, i ^ bit) for i in range(count)])


def total_tensor(value):
    if lax.axis_size("tensor") == 2:
        return value + lax.ppermute(value, "tensor", [(0, 1), (1, 0)])
    return lax.psum(value, "tensor")


def round_end(*values):
    return lax.optimization_barrier(values)


def places(bits):
    found = [0]
    for bit in bits:
        found = found + [i ^ bit for i in found]
    return found


def send_half(piece, bit):
    half = piece.shape[0] // 2
    arrived = across(piece[half:], bit)
    return (piece[:half].astype(jnp.float32) + arrived.astype(jnp.float32)).astype(piece.dtype)


def small_inverse(block):
    side = block.shape[0]
    rows = lax.broadcasted_iota(jnp.int32, (side, 1), 0)
    lanes = lax.broadcasted_iota(jnp.int32, (side, side), 1)
    eye = (lax.broadcasted_iota(jnp.int32, (side, side), 0) == lanes).astype(jnp.float32)
    work = jnp.concatenate([block, eye], axis=1)
    scale = jnp.zeros((side, 1), jnp.float32)
    for j in range(side):
        row = work[j : j + 1, :]
        pivot = row[:, j : j + 1]
        scale = jnp.where(rows == j, lax.rsqrt(pivot), scale)
        work = work - jnp.where(rows > j, work[:, j : j + 1], 0.0) * (row * (1.0 / pivot))
    return work[:, side:] * scale


def lower_inverse_kernel(matrix_ref, out_ref, left_ref):
    size = matrix_ref.shape[0]
    side = min(64, size)
    out_ref[...] = jnp.zeros(out_ref.shape, jnp.float32)
    left_ref[...] = matrix_ref[...]
    for k in range(0, size, side):
        own = pl.ds(k, side)
        block = small_inverse(left_ref[own, k : k + side])
        if k:
            out_ref[own, :k] = -mul(block, mul(left_ref[own, :k], out_ref[:k, :k]))
        out_ref[own, k : k + side] = block
        if k + side < size:
            rest = pl.ds(k + side, size - k - side)
            lower = mul(left_ref[rest, k : k + side], block, ((1,), (1,)))
            left_ref[rest, k : k + side] = lower
            left_ref[rest, k + side :] = left_ref[rest, k + side :] - mul(lower, lower, ((1,), (1,)))


def lower_inverse(matrix):
    return pl.pallas_call(
        lower_inverse_kernel,
        out_shape=jax.ShapeDtypeStruct(matrix.shape, jnp.float32),
        scratch_shapes=[pltpu.VMEM(matrix.shape, jnp.float32)],
        compiler_params=pltpu.CompilerParams(vmem_limit_bytes=16 * megabyte),
        cost_estimate=pl.CostEstimate(flops=10**8, bytes_accessed=10**6, transcendentals=0),
        name="lower_inverse",
    )(matrix)


def chosen(activations, depth, rels, start, size):
    me = lax.axis_index("dp")
    own = activations.shape[0]
    source = jnp.asarray(rels, jnp.int32) ^ me
    if depth % 128 or size % 128:
        blocks = activations.reshape(own, -1, depth)[:, :, start : start + size]
        return jnp.take(blocks, source, axis=1).transpose(1, 0, 2)

    def kernel(source_ref, block_ref, out_ref):
        out_ref[0] = block_ref[:, start : start + size]

    return pl.pallas_call(
        kernel,
        grid_spec=pltpu.PrefetchScalarGridSpec(
            num_scalar_prefetch=1,
            grid=(len(rels),),
            in_specs=[pl.BlockSpec((own, depth), lambda i, source_ref: (0, source_ref[i]))],
            out_specs=pl.BlockSpec((1, own, size), lambda i, source_ref: (i, 0, 0)),
        ),
        out_shape=jax.ShapeDtypeStruct((len(rels), own, size), activations.dtype),
        compiler_params=pltpu.CompilerParams(vmem_limit_bytes=16 * megabyte),
        cost_estimate=pl.CostEstimate(flops=0, bytes_accessed=12 * 10**6, transcendentals=0),
        name="chosen",
    )(source, activations)


def partials(left, activations, depth, rels, cuts, orders, paired=None):
    me = lax.axis_index("dp")
    own = activations.shape[0]
    rank = left.shape[0]
    if depth % 128 or any(size % 128 for _, size in cuts):
        outs = []
        for (start, size), order in zip(cuts, orders):
            rows = chosen(activations, depth, [rels[p] for p in order], start, size)
            term = jnp.einsum("kt,rtb->rkb", left, rows, preferred_element_type=jnp.float32)
            if paired is not None:
                term = term + jnp.einsum("kt,rtb->rkb", paired[0], paired[1][jnp.asarray(order)], preferred_element_type=jnp.float32)
            outs.append(term.astype(jnp.bfloat16))
        return outs
    source = jnp.asarray(rels, jnp.int32) ^ me
    goes = jnp.asarray([[order.index(i) for i in range(len(rels))] for order in orders], jnp.int32)

    def kernel(source_ref, goes_ref, left_ref, block_ref, *refs):
        if paired is not None:
            other_left_ref, other_ref, *out_refs = refs
        else:
            out_refs = refs
        for (start, size), out_ref in zip(cuts, out_refs):
            term = jnp.dot(left_ref[...], block_ref[:, start : start + size], preferred_element_type=jnp.float32)
            if paired is not None:
                term = term + jnp.dot(other_left_ref[...], other_ref[0], preferred_element_type=jnp.float32)
            out_ref[0] = term.astype(out_ref.dtype)

    def out_spec(c, size):
        return pl.BlockSpec((1, rank, size), lambda i, source_ref, goes_ref: (goes_ref[c, i], 0, 0))

    in_specs = [
        pl.BlockSpec(left.shape, lambda i, source_ref, goes_ref: (0, 0)),
        pl.BlockSpec((own, depth), lambda i, source_ref, goes_ref: (0, source_ref[i])),
    ]
    operands = [left, activations]
    if paired is not None:
        in_specs += [
            pl.BlockSpec(left.shape, lambda i, source_ref, goes_ref: (0, 0)),
            pl.BlockSpec((1,) + paired[1].shape[1:], lambda i, source_ref, goes_ref: (i, 0, 0)),
        ]
        operands += list(paired)
    return pl.pallas_call(
        kernel,
        grid_spec=pltpu.PrefetchScalarGridSpec(
            num_scalar_prefetch=2,
            grid=(len(rels),),
            in_specs=in_specs,
            out_specs=[out_spec(c, size) for c, (_, size) in enumerate(cuts)],
        ),
        out_shape=[jax.ShapeDtypeStruct((len(rels), rank, size), jnp.bfloat16) for _, size in cuts],
        compiler_params=pltpu.CompilerParams(vmem_limit_bytes=24 * megabyte),
        cost_estimate=pl.CostEstimate(flops=4 * 10**9, bytes_accessed=25 * 10**6, transcendentals=0),
        name="partials",
    )(source, goes, *operands)


def correct(weights, gradient, halves, cuts, half_orders, last_bits):
    count = lax.axis_size("dp")
    me = lax.axis_index("dp")
    width = gradient.shape[1]
    rank = weights.shape[0]
    depth = gradient.shape[0] // count
    source = jnp.arange(count, dtype=jnp.int32) ^ me
    position = jnp.asarray(
        [[order.index(i & ~bit) for i in range(count)] for order, bit in zip(half_orders, last_bits)], jnp.int32
    )

    def kernel(source_ref, position_ref, weights_ref, gradient_ref, *refs):
        out_ref = refs[-1]
        step = pl.program_id(0)
        for c, ((start, size), bit) in enumerate(zip(cuts, last_bits)):
            rows = pl.ds(start, size)
            factor = jnp.where((step & bit) == 0, refs[2 * c][0], refs[2 * c + 1][0])
            term = jnp.dot(factor, weights_ref[...], preferred_element_type=jnp.float32)
            out_ref[rows, :] = (gradient_ref[rows, :].astype(jnp.float32) - term).astype(out_ref.dtype)

    def half_spec(c, size):
        return pl.BlockSpec((1, size, rank), lambda i, source_ref, position_ref: (position_ref[c, i], 0, 0))

    block = pl.BlockSpec((depth, width), lambda i, source_ref, position_ref: (source_ref[i], 0))
    return pl.pallas_call(
        kernel,
        grid_spec=pltpu.PrefetchScalarGridSpec(
            num_scalar_prefetch=2,
            grid=(count,),
            in_specs=[pl.BlockSpec((rank, width), lambda i, source_ref, position_ref: (0, 0)), block]
            + [half_spec(c, size) for c, (_, size) in enumerate(cuts) for _ in range(2)],
            out_specs=block,
        ),
        out_shape=jax.ShapeDtypeStruct(gradient.shape, gradient.dtype),
        compiler_params=pltpu.CompilerParams(vmem_limit_bytes=40 * megabyte),
        cost_estimate=pl.CostEstimate(flops=7 * 10**9, bytes_accessed=80 * 10**6, transcendentals=0),
        name="correct",
    )(source, position, weights, gradient, *halves)


def cut(extent, shares):
    unit = extent // sum(shares)
    out, start = [], 0
    for i, share in enumerate(shares):
        size = unit * share if i + 1 < len(shares) else extent - start
        out.append((start, size))
        start += size
    return out


def local(activations, test_matrix, gradient):
    count = lax.axis_size("dp")
    me = lax.axis_index("dp")
    own, hidden = activations.shape
    tokens = own * count
    probes = test_matrix.shape[1]
    rank = probes * count
    depth = hidden // count
    width = gradient.shape[1]
    bx, by, bl = 1, 2, 4
    lead = [1 << i for i in range(3, count.bit_length() - 1)][::-1]
    every = list(range(count))
    rotations = ((bx, by, bl), (by, bl, bx), (bl, bx, by))

    parts = cut(depth, (3, 3, 2, 2, 3))
    without = [[r for r in every if not r & bit] for bit in (bx, by)]
    with_bit = [[r | bit for r in rs] for rs, bit in zip(without, (bx, by))]

    give = [chosen(activations, depth, rels, *part) for rels, part in zip(with_bit, parts[:2])]
    probe_rows = test_matrix.T
    swapped = [across(value, bit) for value, bit in zip(give, (bx, by))]
    for bit in lead:
        probe_rows = jnp.concatenate([probe_rows, across(probe_rows, bit)], axis=0)
    probe_rows, *swapped = round_end(probe_rows, *swapped)
    strips = cut(hidden, (69, 69, 70))
    held = [probe_rows[:, start : start + size] for start, size in strips]
    for step in (0, 1):
        arrived = [across(value, order[step]) for value, order in zip(held, rotations)]
        held = [jnp.concatenate([a, b], axis=0) for a, b in zip(held, arrived)]
        held = round_end(*held)
    arrived = [across(value, order[2]) for value, order in zip(held, rotations)]

    def sketch_of(rows):
        return [
            low_mul(activations[:, start : start + size], value, ((1,), (1,)))
            for value, (start, size) in zip(rows, strips)
        ]

    early = sketch_of(held)
    gradient_blocks = gradient.reshape(count, depth, width)
    arrived = round_end(*arrived, *early)
    early, arrived = arrived[3:], arrived[:3]
    late = sketch_of(arrived)
    sketch = 0.0
    for order, first, second in zip(rotations, early, late):
        source = jnp.asarray(places(lead + list(order)), jnp.int32) ^ me
        columns = jnp.repeat(source, probes) * probes + jnp.tile(jnp.arange(probes), count)
        spread = (columns[:, None] == jnp.arange(rank)).astype(jnp.float32)
        sketch = sketch + mul(jnp.concatenate([first, second], axis=1), spread)
    sketch = total_tensor(sketch)
    sketch_low = sketch.astype(jnp.bfloat16)
    left = sketch_low.T

    orders = [lead + [bl, by], lead + [bl, bx], lead + [bl, by, bx], lead + [bl, bx, by], lead + [by, bx, bl]]
    places_of = [places(order) for order in orders]
    other_left = [across(left, bit) for bit in (bx, by)]
    pieces = list(partials(left, activations, depth, every, parts[2:], places_of[2:]))
    for i, bit in enumerate((bx, by)):
        slot = [without[i].index(r) for r in places_of[i]]
        pieces[i:i] = partials(
            left, activations, depth, without[i], parts[i : i + 1], [slot], (other_left[i], swapped[i])
        )
    core = mul(sketch, sketch_low.astype(jnp.float32), ((0,), (0,)))
    steps = [list(reversed(order)) for order in orders]
    turn = 0
    while any(steps):
        pieces = [send_half(piece, step.pop(0)) if step else piece for piece, step in zip(pieces, steps)]
        if turn == 0:
            for bit in [bx, by, bl] + lead:
                core = core + across(core, bit)
        turn += 1
        if any(steps):
            *pieces, core = round_end(*pieces, core)
    core = core / tokens
    core = 0.5 * (core + core.T)
    columns = jnp.concatenate([piece[0].astype(jnp.float32) for piece in pieces], axis=1) / tokens
    moment = mul(columns, columns, ((1,), (1,)))
    rows = columns.astype(jnp.bfloat16).T[None]
    rows, moment, core = round_end(rows, moment, core)

    for bit in lead:
        rows = jnp.concatenate([rows, across(rows, bit)], axis=0)
    for bit in [bx, by, bl] + lead:
        moment = moment + across(moment, bit)
    moment = total_tensor(moment)
    shares = cut(depth, (4, 4, 5))
    half_orders = [places(lead + list(order[:2])) for order in rotations]

    def facing(c, with_last):
        start, size = shares[c]
        source = jnp.asarray([r ^ (rotations[c][2] if with_last else 0) for r in half_orders[c]], jnp.int32) ^ me
        return jnp.take(gradient_blocks[:, start : start + size], source, axis=0)

    near = [facing(c, False) for c in range(3)]
    rows, moment, core, *near = round_end(rows, moment, core, *near)
    held = [rows[:, start : start + size] for start, size in shares]
    arrived = [across(value, order[0]) for value, order in zip(held, rotations)]
    held = [jnp.concatenate([a, b], axis=0) for a, b in zip(held, arrived)]
    *held, moment, core = round_end(*held, moment, core)
    arrived = [across(value, order[1]) for value, order in zip(held, rotations)]
    inverse = lower_inverse(core)
    held = [jnp.concatenate([a, b], axis=0) for a, b in zip(held, arrived)]
    *held, moment, inverse = round_end(*held, moment, inverse)
    arrived = [across(value, order[2]) for value, order in zip(held, rotations)]
    gram = mul(mul(inverse, moment), inverse, ((1,), (1,)))
    damping = damping_ratio * jnp.trace(gram) / rank
    step = mul(lower_inverse(gram + damping * jnp.eye(rank, dtype=jnp.float32)), inverse)
    solver = mul(step, step, ((0,), (0,)))

    def project(factors, facings):
        total = 0.0
        for factor, value in zip(factors, facings):
            total = total + low_mul(factor.reshape(-1, rank), value.reshape(-1, width), ((0,), (0,)))
        return total

    projected = project(held, near)
    far = [facing(c, True) for c in range(3)]
    ended = round_end(*arrived, *far, *held, solver, projected, gram)
    arrived, far, held = ended[:3], ended[3:6], ended[6:9]
    solver, projected, gram = ended[9:]
    projected = total_tensor(projected + project(arrived, far))
    weights = mul(solver, projected).astype(jnp.bfloat16)
    halves = [value for pair in zip(held, arrived) for value in pair]
    out = correct(weights, gradient, halves, shares, half_orders, [order[2] for order in rotations])
    return out, gram


def solution(mesh):
    placed = (P("dp", "tensor"), P("tensor", "dp"), P("tensor", "dp"))
    return jax.shard_map(
        local, mesh=mesh, in_specs=placed, out_specs=(P("tensor", "dp"), P()), check_vma=False
    )
```

```python
import jax
import jax.numpy as jnp
from jax import lax
from jax.experimental import pallas as pl
from jax.experimental.pallas import tpu as pltpu
from jax.sharding import PartitionSpec as P

damping_ratio = 0.1
exact = lax.Precision.HIGHEST
megabyte = 1024 * 1024


def mul(a, b, dims=((1,), (0,))):
    return lax.dot_general(a, b, (dims, ((), ())), precision=exact, preferred_element_type=jnp.float32)


def low_mul(a, b, dims=((1,), (0,))):
    return lax.dot_general(a, b, (dims, ((), ())), preferred_element_type=jnp.float32)


def across(value, bit):
    count = lax.axis_size("dp")
    return lax.ppermute(value, "dp", [(i, i ^ bit) for i in range(count)])


def total_tensor(value):
    return value + other_core(value) if two_cores() else lax.psum(value, "tensor")


def two_cores():
    return lax.axis_size("tensor") == 2


def my_half(value, other=False):
    half = value.shape[0] // 2
    core = lax.axis_index("tensor")
    return lax.dynamic_slice_in_dim(value, (1 - core if other else core) * half, half, axis=0)


def other_core(value):
    return lax.ppermute(value, "tensor", [(0, 1), (1, 0)])


def both_halves(mine):
    theirs = other_core(mine)
    first = lax.axis_index("tensor") == 0
    return jnp.concatenate([jnp.where(first, mine, theirs), jnp.where(first, theirs, mine)], axis=0)


def round_end(*values):
    return lax.optimization_barrier(values)


def places(bits):
    found = [0]
    for bit in bits:
        found = found + [i ^ bit for i in found]
    return found


def small_inverse(block):
    side = block.shape[0]
    rows = lax.broadcasted_iota(jnp.int32, (side, 1), 0)
    lanes = lax.broadcasted_iota(jnp.int32, (side, side), 1)
    eye = (lax.broadcasted_iota(jnp.int32, (side, side), 0) == lanes).astype(jnp.float32)
    work = jnp.concatenate([block, eye], axis=1)
    scale = jnp.zeros((side, 1), jnp.float32)
    for j in range(side):
        row = work[j : j + 1, :]
        pivot = row[:, j : j + 1]
        scale = jnp.where(rows == j, lax.rsqrt(pivot), scale)
        work = work - jnp.where(rows > j, work[:, j : j + 1], 0.0) * (row * (1.0 / pivot))
    return work[:, side:] * scale


def lower_inverse_kernel(matrix_ref, out_ref, left_ref):
    size = matrix_ref.shape[0]
    side = min(64, size)
    out_ref[...] = jnp.zeros(out_ref.shape, jnp.float32)
    left_ref[...] = matrix_ref[...]
    for k in range(0, size, side):
        own = pl.ds(k, side)
        block = small_inverse(left_ref[own, k : k + side])
        if k:
            out_ref[own, :k] = -mul(block, mul(left_ref[own, :k], out_ref[:k, :k]))
        out_ref[own, k : k + side] = block
        if k + side < size:
            rest = pl.ds(k + side, size - k - side)
            lower = mul(left_ref[rest, k : k + side], block, ((1,), (1,)))
            left_ref[rest, k : k + side] = lower
            left_ref[rest, k + side :] = left_ref[rest, k + side :] - mul(lower, lower, ((1,), (1,)))


def lower_inverse(matrix):
    return pl.pallas_call(
        lower_inverse_kernel,
        out_shape=jax.ShapeDtypeStruct(matrix.shape, jnp.float32),
        scratch_shapes=[pltpu.VMEM(matrix.shape, jnp.float32)],
        compiler_params=pltpu.CompilerParams(vmem_limit_bytes=4 * megabyte),
        cost_estimate=pl.CostEstimate(flops=10**8, bytes_accessed=10**6, transcendentals=0),
        name="lower_inverse",
    )(matrix)


def aligned(depth, sizes):
    return depth % 128 == 0 and all(size % 128 == 0 for size in sizes)


def taken(activations, depth, rels, start, size):
    blocks = activations.reshape(activations.shape[0], -1, depth)[:, :, start : start + size]
    return jnp.take(blocks, jnp.asarray(rels, jnp.int32) ^ lax.axis_index("dp"), axis=1).transpose(1, 0, 2)


def chosen(activations, depth, rels, cuts):
    if not aligned(depth, [size for _, size in cuts]):
        return [taken(activations, depth, own, *part) for own, part in zip(rels, cuts)]
    own = activations.shape[0]
    here = lax.axis_index("dp")[None]

    def kernel(here_ref, in_ref, *refs):
        out_refs, sems = refs[:-1], refs[-1]
        copies = []
        for c, (start, size) in enumerate(cuts):
            for i, rel in enumerate(rels[c]):
                at = pl.multiple_of((here_ref[0] ^ rel) * depth + start, 128)
                source = in_ref.at[:, pl.ds(at, size)]
                copies.append(pltpu.make_async_copy(source, out_refs[c].at[i], sems.at[c, i]))
        for copy in copies:
            copy.start()
        for copy in copies:
            copy.wait()

    anywhere = pl.BlockSpec(memory_space=pl.ANY)
    return pl.pallas_call(
        kernel,
        in_specs=[pl.BlockSpec(memory_space=pltpu.SMEM), anywhere],
        out_specs=[pl.BlockSpec(memory_space=pltpu.VMEM)] * len(cuts),
        out_shape=[jax.ShapeDtypeStruct((len(rels[0]), own, size), activations.dtype) for _, size in cuts],
        scratch_shapes=[pltpu.SemaphoreType.DMA((len(cuts), len(rels[0])))],
        compiler_params=pltpu.CompilerParams(vmem_limit_bytes=56 * megabyte),
        cost_estimate=pl.CostEstimate(flops=0, bytes_accessed=6 * 10**6, transcendentals=0),
        name="chosen",
    )(here, activations)


def partials(left, activations, depth, rels, cuts, paired):
    rank = left.shape[0]
    if not aligned(depth, [size for _, size in cuts]):
        outs = []
        for own, part, pair in zip(rels, cuts, paired):
            rows = taken(activations, depth, own, *part)
            term = jnp.einsum("kt,rtb->rkb", left, rows, preferred_element_type=jnp.float32)
            if pair is not None:
                term = term + jnp.einsum("kt,rtb->rkb", pair[0], pair[1], preferred_element_type=jnp.float32)
            outs.append(term.astype(jnp.bfloat16))
        return outs
    source = jnp.asarray(rels, jnp.int32) ^ lax.axis_index("dp")
    pairs = [pair for pair in paired if pair is not None]

    def kernel(source_ref, left_ref, block_ref, *refs):
        others = list(refs[: 2 * len(pairs)])
        for c, ((start, size), pair) in enumerate(zip(cuts, paired)):
            out_ref = refs[2 * len(pairs) + c]
            other_left_ref, other_ref = (others.pop(0), others.pop(0)) if pair is not None else (None, None)

            def one(i, carry):
                at = pl.multiple_of(source_ref[c, i] * depth + start, 128)
                term = jnp.dot(left_ref[...], block_ref[:, pl.ds(at, size)], preferred_element_type=jnp.float32)
                if other_ref is not None:
                    term = term + jnp.dot(other_left_ref[...], other_ref[i], preferred_element_type=jnp.float32)
                out_ref[i] = term.astype(out_ref.dtype)
                return carry

            lax.fori_loop(0, len(rels[c]), one, 0)

    vmem = pl.BlockSpec(memory_space=pltpu.VMEM)
    return pl.pallas_call(
        kernel,
        in_specs=[pl.BlockSpec(memory_space=pltpu.SMEM)] + [vmem] * (2 + 2 * len(pairs)),
        out_specs=[vmem] * len(cuts),
        out_shape=[jax.ShapeDtypeStruct((len(rels[0]), rank, size), jnp.bfloat16) for _, size in cuts],
        compiler_params=pltpu.CompilerParams(vmem_limit_bytes=24 * megabyte),
        cost_estimate=pl.CostEstimate(flops=10**9, bytes_accessed=5 * 10**6, transcendentals=0),
        name="partials",
    )(source, left, activations, *[value for pair in pairs for value in pair])


def finish(kept, arrived, tokens):
    rank = kept[0].shape[1]
    sizes = [value.shape[2] for value in kept]
    depth = sum(sizes)
    if not aligned(depth, sizes):
        columns = [a[0].astype(jnp.float32) + b[0].astype(jnp.float32) for a, b in zip(kept, arrived)]
        columns = jnp.concatenate(columns, axis=1) / tokens
        return columns.astype(jnp.bfloat16).T, mul(columns, columns, ((1,), (1,)))

    def kernel(*refs):
        rows_ref, moment_ref = refs[-2:]
        start, moment = 0, 0.0
        for c, size in enumerate(sizes):
            columns = (refs[c][0].astype(jnp.float32) + refs[len(sizes) + c][0].astype(jnp.float32)) * (1.0 / tokens)
            moment = moment + mul(columns, columns, ((1,), (1,)))
            rows_ref[start : start + size, :] = columns.T.astype(rows_ref.dtype)
            start += size
        moment_ref[...] = moment

    return pl.pallas_call(
        kernel,
        out_shape=[
            jax.ShapeDtypeStruct((depth, rank), jnp.bfloat16),
            jax.ShapeDtypeStruct((rank, rank), jnp.float32),
        ],
        compiler_params=pltpu.CompilerParams(vmem_limit_bytes=10 * megabyte),
        cost_estimate=pl.CostEstimate(flops=10**9, bytes_accessed=3 * 10**6, transcendentals=0),
        name="finish",
    )(*kept, *arrived)


def project(me, gradient, total, factors, rels, starts, depth):
    rank, width = factors[0].shape[2], gradient.shape[1]

    tallest = max(value.shape[0] * value.shape[1] for value in factors)

    def kernel(me_ref, total_ref, gradient_ref, *refs):
        ins, (out_ref, held, facing, sems) = refs[: len(factors)], refs[len(factors) :]

        def fetch(q):
            size = factors[q].shape[1]
            out = []
            for b, rel in enumerate(rels[q]):
                at = pl.multiple_of((me_ref[0] ^ rel) * depth + starts[q], 16)
                rows = pl.ds(b * size, size)
                out.append(pltpu.make_async_copy(ins[q].at[b], held.at[q % 3, rows], sems.at[q % 3, 2 * b]))
                source = gradient_ref.at[pl.ds(at, size)]
                out.append(pltpu.make_async_copy(source, facing.at[q % 3, rows], sems.at[q % 3, 2 * b + 1]))
            return out

        for q in range(min(2, len(factors))):
            for copy in fetch(q):
                copy.start()
        out_ref[...] = total_ref[...]
        for q, factor in enumerate(factors):
            for copy in fetch(q):
                copy.wait()
            if q + 2 < len(factors):
                for copy in fetch(q + 2):
                    copy.start()
            rows = slice(0, factor.shape[0] * factor.shape[1])
            out_ref[...] += low_mul(held[q % 3, rows, :], facing[q % 3, rows, :], ((0,), (0,)))

    return pl.pallas_call(
        kernel,
        in_specs=[pl.BlockSpec(memory_space=pltpu.SMEM), pl.BlockSpec(memory_space=pltpu.VMEM)]
        + [pl.BlockSpec(memory_space=pl.ANY)] * (1 + len(factors)),
        out_specs=pl.BlockSpec(memory_space=pltpu.VMEM),
        out_shape=jax.ShapeDtypeStruct((rank, width), jnp.float32),
        scratch_shapes=[
            pltpu.VMEM((3, tallest, rank), factors[0].dtype),
            pltpu.VMEM((3, tallest, width), gradient.dtype),
            pltpu.SemaphoreType.DMA((3, 2 * max(len(own) for own in rels))),
        ],
        compiler_params=pltpu.CompilerParams(vmem_limit_bytes=28 * megabyte),
        cost_estimate=pl.CostEstimate(flops=10**8, bytes_accessed=10**6, transcendentals=0),
        name="project",
    )(me, total, gradient, *factors)


def correct(me, solver, projected, gradient, factors, rels, cuts, part_of, depth):
    rank, width = projected[0].shape
    blocks = gradient.shape[0] // depth
    tile = max(t for t in range(16, min(depth, 512) + 1, 16) if depth % t == 0)
    found = {(part_of[q], rel): (q, b) for q in range(len(factors)) for b, rel in enumerate(rels[q])}

    def kernel(me_ref, solver_ref, *refs):
        projected_refs, (gradient_ref, *refs) = refs[: len(projected)], refs[len(projected) :]
        ins, (out_ref, weights_ref, held, facing, done, in_sems, out_sems) = refs[: len(factors)], refs[len(factors) :]

        def base(i):
            return pl.multiple_of((me_ref[0] ^ i) * depth, 16)

        def fetch(i):
            whole = gradient_ref.at[pl.ds(base(i), depth)]
            out = [pltpu.make_async_copy(whole, facing.at[i % 3], in_sems.at[i % 3, len(cuts)])]
            for c, (start, size) in enumerate(cuts):
                q, b = found[c, i]
                into = held.at[i % 3, pl.ds(start, size)]
                out.append(pltpu.make_async_copy(ins[q].at[b], into, in_sems.at[i % 3, c]))
            return out

        def store(i):
            return pltpu.make_async_copy(done.at[i % 2], out_ref.at[pl.ds(base(i), depth)], out_sems.at[i % 2])

        for i in range(min(2, blocks)):
            for copy in fetch(i):
                copy.start()
        total = projected_refs[0][...]
        for ref in projected_refs[1:]:
            total = total + ref[...]
        weights_ref[...] = mul(solver_ref[...], total).astype(weights_ref.dtype)
        for i in range(blocks):
            for copy in fetch(i):
                copy.wait()
            if i + 2 < blocks:
                for copy in fetch(i + 2):
                    copy.start()
            if i >= 2:
                store(i - 2).wait()

            def one(t, carry):
                rows = pl.ds(pl.multiple_of(t * tile, 16), tile)
                term = jnp.dot(held[i % 3, rows, :], weights_ref[...], preferred_element_type=jnp.float32)
                done[i % 2, rows, :] = (facing[i % 3, rows, :].astype(jnp.float32) - term).astype(done.dtype)
                return carry

            lax.fori_loop(0, depth // tile, one, 0)
            store(i).start()
        for i in range(max(0, blocks - 2), blocks):
            store(i).wait()

    vmem = pl.BlockSpec(memory_space=pltpu.VMEM)
    return pl.pallas_call(
        kernel,
        in_specs=[pl.BlockSpec(memory_space=pltpu.SMEM)]
        + [vmem] * (1 + len(projected))
        + [pl.BlockSpec(memory_space=pl.ANY)] * (1 + len(factors)),
        out_specs=pl.BlockSpec(memory_space=pl.ANY),
        out_shape=jax.ShapeDtypeStruct(gradient.shape, gradient.dtype),
        scratch_shapes=[
            pltpu.VMEM((rank, width), jnp.bfloat16),
            pltpu.VMEM((3, depth, rank), jnp.bfloat16),
            pltpu.VMEM((3, depth, width), gradient.dtype),
            pltpu.VMEM((2, depth, width), gradient.dtype),
            pltpu.SemaphoreType.DMA((3, len(cuts) + 1)),
            pltpu.SemaphoreType.DMA((2,)),
        ],
        compiler_params=pltpu.CompilerParams(vmem_limit_bytes=32 * megabyte),
        cost_estimate=pl.CostEstimate(flops=7 * 10**9, bytes_accessed=70 * 10**6, transcendentals=0),
        name="correct",
    )(me, solver, *projected, gradient, *factors)


def cut(extent, shares):
    unit = extent // sum(shares)
    out, start = [], 0
    for i, share in enumerate(shares):
        size = unit * share if i + 1 < len(shares) else extent - start
        out.append((start, size))
        start += size
    return out


def split_pairs(values, groups=2):
    size = len(values) // groups
    return [list(values[i * size : (i + 1) * size]) for i in range(groups)]


def local(activations, test_matrix, gradient):
    count = lax.axis_size("dp")
    me = lax.axis_index("dp")
    own, hidden = activations.shape
    tokens = own * count
    probes = test_matrix.shape[1]
    rank = probes * count
    depth = hidden // count
    bx, by, bl = 1, 2, 4
    lead = [1 << i for i in range(3, count.bit_length() - 1)][::-1]
    every = list(range(count))
    rotations = ((bx, by, bl), (by, bl, bx), (bl, bx, by))

    parts = cut(depth, (4, 4, 3, 1, 1))
    orders = [
        lead + [bl, by],
        lead + [bx, bl],
        lead + [bl, by, bx],
        [by, bx] + lead + [bl],
        lead + [bl, bx, by],
    ]
    swaps = (bx, by)

    probe_rows = test_matrix.T
    give = chosen(activations, depth, [[r | bit for r in places(order)] for order, bit in zip(orders, swaps)], parts[:2])
    swapped = [across(value, bit) for value, bit in zip(give, swaps)]
    for bit in lead:
        probe_rows = jnp.concatenate([probe_rows, across(probe_rows, bit)], axis=0)
    probe_rows, *swapped = round_end(probe_rows, *swapped)
    strips = cut(hidden, (69, 69, 70))
    first = [probe_rows[:, start : start + size] for start, size in strips]
    arrived = [across(value, order[0]) for value, order in zip(first, rotations)]
    first = [jnp.concatenate(pair, axis=0) for pair in zip(first, arrived)]
    first = round_end(*first)
    second = [across(value, order[1]) for value, order in zip(first, rotations)]
    first, second = split_pairs(round_end(*first, *second))

    def sketch_of(strip, rows):
        start, size = strip
        return low_mul(activations[:, start : start + size], rows, ((1,), (1,)))

    third = [across(value, order[2]) for value, order in zip(first, rotations)]
    terms = [[sketch_of(strip, jnp.concatenate(pair, axis=0))] for strip, pair in zip(strips, zip(first, second))]
    ended = round_end(*third, *second, *[value for term in terms for value in term])
    third, second, terms = split_pairs(ended, 3)
    terms = [[value] for value in terms]
    fourth = [across(value, order[2]) for value, order in zip(second, rotations)]
    for term, strip, value in zip(terms, strips, third):
        term.append(sketch_of(strip, value))
    *fourth, terms = [*round_end(*fourth, *[value for term in terms for value in term])[: len(strips)], terms]
    for term, strip, value in zip(terms, strips, fourth):
        term.append(sketch_of(strip, value))
    spread = []
    for order in rotations:
        source = jnp.asarray(places(lead + list(order)), jnp.int32) ^ me
        columns = jnp.repeat(source, probes) * probes + jnp.tile(jnp.arange(probes), count)
        spread.append((columns[:, None] == jnp.arange(rank)).astype(jnp.float32))
    terms = [value for term in terms for value in term]
    sketch = total_tensor(mul(jnp.concatenate(terms, axis=1), jnp.concatenate(spread, axis=0)))
    sketch_low = sketch.astype(jnp.bfloat16)
    left = sketch_low.T

    steps = [list(reversed(order)) for order in orders]
    rels = [places(order) for order in orders]
    half = [len(order) // 2 for order in rels]
    pairs = [None] * len(parts)
    sent, kept = [None] * len(parts), [None] * len(parts)
    for c in range(2, len(parts)):
        (sent[c],) = partials(left, activations, depth, [rels[c][half[c] :]], [parts[c]], [None])
    other_left = [across(left, bit) for bit in swaps]
    *other_left, sent[2] = round_end(*other_left, sent[2])
    for c in range(2):
        pair = (other_left[c], swapped[c])
        (sent[c],) = partials(
            left, activations, depth, [rels[c][half[c] :]], [parts[c]], [(pair[0], pair[1][half[c] :])]
        )
        pairs[c] = (pair[0], pair[1][: half[c]])
    kept[2:] = partials(
        left, activations, depth, [rels[c][: half[c]] for c in range(2, len(parts))], parts[2:], pairs[2:]
    )
    kept[:2] = partials(left, activations, depth, [rels[c][: half[c]] for c in range(2)], parts[:2], pairs[:2])
    core = mul(sketch, sketch_low.astype(jnp.float32), ((0,), (0,)))
    core = my_half(core) if two_cores() else core
    turn = 0
    while True:
        arrived = [across(sent[c], step[0]) if step else None for c, step in enumerate(steps)]
        for bit in (lead, [], [bx, by], [bl], [])[min(turn, 4)]:
            core = core + across(core, bit)
        turn += 1
        for c, step in enumerate(steps):
            if len(step) > 1:
                cutting = kept[c].shape[0] // 2
                total = [
                    kept[c][rows].astype(jnp.float32) + arrived[c][rows].astype(jnp.float32)
                    for rows in (slice(cutting, None), slice(0, cutting))
                ]
                sent[c], kept[c] = [value.astype(jnp.bfloat16) for value in total]
                step.pop(0)
            elif step:
                sent[c] = arrived[c]
                step.pop(0)
        *ended, core = round_end(*sent, *kept, core)
        sent, kept = split_pairs(ended)
        if not any(steps):
            break
    rows, moment = finish(kept, sent, tokens)
    core = (both_halves(core) if two_cores() else core) / tokens
    core = 0.5 * (core + core.T)

    rows = rows[None]
    for bit in lead:
        rows = jnp.concatenate([rows, across(rows, bit)], axis=0)
    if two_cores():
        moment = my_half(moment) + other_core(my_half(moment, other=True))
    for bit in [bx, by, bl]:
        moment = moment + across(moment, bit)
    inverse = lower_inverse(core)
    rows, moment, inverse = round_end(rows, moment, inverse)
    shares = cut(depth, (4, 4, 5))
    first = [rows[:, start : start + size] for start, size in shares]
    arrived = [across(value, order[0]) for value, order in zip(first, rotations)]
    for bit in lead:
        moment = moment + across(moment, bit)
    moment = both_halves(moment) if two_cores() else lax.psum(moment, "tensor")
    first = [jnp.concatenate(pair, axis=0) for pair in zip(first, arrived)]
    *first, moment = round_end(*first, moment)
    second = [across(value, order[1]) for value, order in zip(first, rotations)]
    gram = mul(mul(inverse, moment), inverse, ((1,), (1,)))
    damping = damping_ratio * jnp.trace(gram) / rank
    last = lower_inverse(gram + damping * jnp.eye(rank, dtype=jnp.float32))
    *both, gram, last = round_end(*first, *second, gram, last)
    first, second = split_pairs(both)
    starts = [start for start, _ in shares]
    near = [places(lead + [order[0]]) for order in rotations]
    next_to = [[r ^ order[1] for r in rs] for rs, order in zip(near, rotations)]
    far = [[r ^ order[2] for r in rs] for rs, order in zip(near, rotations)]
    farthest = [[r ^ order[2] for r in rs] for rs, order in zip(next_to, rotations)]
    here = me[None]
    third = [across(value, order[2]) for value, order in zip(first, rotations)]
    step = mul(last, inverse)
    solver = mul(step, step, ((0,), (0,)))
    projected = jnp.zeros((rank, gradient.shape[1]), jnp.float32)
    projected = project(here, gradient, projected, first + second, near + next_to, starts * 2, depth)
    *ended, solver, projected = round_end(*third, *second, solver, projected)
    third, second = split_pairs(ended)
    fourth = [across(value, order[2]) for value, order in zip(second, rotations)]
    projected = project(here, gradient, projected, third, far, starts, depth)
    *fourth, projected = round_end(*fourth, projected)
    projected = project(here, gradient, projected, fourth, farthest, starts, depth)
    projected = (projected, other_core(projected)) if two_cores() else (lax.psum(projected, "tensor"),)
    out = correct(
        here,
        solver,
        projected,
        gradient,
        first + second + third + fourth,
        near + next_to + far + farthest,
        shares,
        [0, 1, 2] * 4,
        depth,
    )
    return out, gram


def solution(mesh):
    placed = (P("dp", "tensor"), P("tensor", "dp"), P("tensor", "dp"))
    return jax.shard_map(
        local, mesh=mesh, in_specs=placed, out_specs=(P("tensor", "dp"), P()), check_vma=False
    )
```

```python
import jax
import jax.numpy as jnp
from jax import lax
from jax.experimental import pallas as pl
from jax.experimental.pallas import tpu as pltpu
from jax.sharding import PartitionSpec as P

damping_ratio = 0.1
exact = lax.Precision.HIGHEST
megabyte = 1024 * 1024


def mul(a, b, dims=((1,), (0,))):
    return lax.dot_general(a, b, (dims, ((), ())), precision=exact, preferred_element_type=jnp.float32)


def low_mul(a, b, dims=((1,), (0,))):
    return lax.dot_general(a, b, (dims, ((), ())), preferred_element_type=jnp.float32)


def across(value, bit):
    count = lax.axis_size("dp")
    return lax.ppermute(value, "dp", [(i, i ^ bit) for i in range(count)])


def total_tensor(value):
    return value + other_core(value) if two_cores() else lax.psum(value, "tensor")


def two_cores():
    return lax.axis_size("tensor") == 2


def my_half(value, other=False):
    half = value.shape[0] // 2
    core = lax.axis_index("tensor")
    return lax.dynamic_slice_in_dim(value, (1 - core if other else core) * half, half, axis=0)


def other_core(value):
    return lax.ppermute(value, "tensor", [(0, 1), (1, 0)])


def both_halves(mine):
    theirs = other_core(mine)
    first = lax.axis_index("tensor") == 0
    return jnp.concatenate([jnp.where(first, mine, theirs), jnp.where(first, theirs, mine)], axis=0)


def round_end(*values):
    return lax.optimization_barrier(values)


def places(bits):
    found = [0]
    for bit in bits:
        found = found + [i ^ bit for i in found]
    return found


def small_inverse(block):
    side = block.shape[0]
    lanes = lax.broadcasted_iota(jnp.int32, (side, side), 1)
    eye = (lax.broadcasted_iota(jnp.int32, (side, side), 0) == lanes).astype(jnp.float32)
    full = jnp.concatenate([block, eye], axis=1)
    work = [full[g : g + 8] for g in range(0, side, 8)]
    pivots = [jnp.ones((8, 1), jnp.float32) for _ in work]
    rows = lax.broadcasted_iota(jnp.int32, (8, 1), 0)
    for j in range(side):
        own, r = divmod(j, 8)
        row = work[own][r : r + 1, :]
        pivot = row[:, j : j + 1]
        pivots[own] = jnp.where(rows == r, pivot, pivots[own])
        unit = row * (1.0 / pivot)
        if r < 7:
            work[own] = work[own] - jnp.where(rows > r, work[own][:, j : j + 1], 0.0) * unit
        for g in range(own + 1, len(work)):
            work[g] = work[g] - work[g][:, j : j + 1] * unit
    return jnp.concatenate([w[:, side:] * lax.rsqrt(p) for w, p in zip(work, pivots)], axis=0)


def lower_inverse_kernel(matrix_ref, out_ref, left_ref):
    size = matrix_ref.shape[0]
    side = min(128, size)
    out_ref[...] = jnp.zeros(out_ref.shape, jnp.float32)
    left_ref[...] = matrix_ref[...]
    for k in range(0, size, side):
        own = pl.ds(k, side)
        block = small_inverse(left_ref[own, k : k + side])
        if k:
            out_ref[own, :k] = -mul(block, mul(left_ref[own, :k], out_ref[:k, :k]))
        out_ref[own, k : k + side] = block
        if k + side < size:
            rest = pl.ds(k + side, size - k - side)
            lower = mul(left_ref[rest, k : k + side], block, ((1,), (1,)))
            left_ref[rest, k : k + side] = lower
            left_ref[rest, k + side :] = left_ref[rest, k + side :] - mul(lower, lower, ((1,), (1,)))


def lower_inverse(matrix):
    return pl.pallas_call(
        lower_inverse_kernel,
        out_shape=jax.ShapeDtypeStruct(matrix.shape, jnp.float32),
        scratch_shapes=[pltpu.VMEM(matrix.shape, jnp.float32)],
        compiler_params=pltpu.CompilerParams(vmem_limit_bytes=12 * megabyte),
        cost_estimate=pl.CostEstimate(flops=10**8, bytes_accessed=10**6, transcendentals=0),
        name="lower_inverse",
    )(matrix)


def aligned(depth, sizes):
    return depth % 128 == 0 and all(size % 128 == 0 for size in sizes)


def taken(activations, depth, rels, start, size):
    blocks = activations.reshape(activations.shape[0], -1, depth)[:, :, start : start + size]
    return jnp.take(blocks, jnp.asarray(rels, jnp.int32) ^ lax.axis_index("dp"), axis=1).transpose(1, 0, 2)


def chosen(activations, depth, rels, cuts):
    if not aligned(depth, [size for _, size in cuts]):
        return [taken(activations, depth, own, *part) for own, part in zip(rels, cuts)]
    own = activations.shape[0]
    here = lax.axis_index("dp")[None]

    def kernel(here_ref, in_ref, *refs):
        out_refs, sems = refs[:-1], refs[-1]
        copies = []
        for c, (start, size) in enumerate(cuts):
            for i, rel in enumerate(rels[c]):
                at = pl.multiple_of((here_ref[0] ^ rel) * depth + start, 128)
                source = in_ref.at[:, pl.ds(at, size)]
                copies.append(pltpu.make_async_copy(source, out_refs[c].at[i], sems.at[c, i]))
        for copy in copies:
            copy.start()
        for copy in copies:
            copy.wait()

    anywhere = pl.BlockSpec(memory_space=pl.ANY)
    return pl.pallas_call(
        kernel,
        in_specs=[pl.BlockSpec(memory_space=pltpu.SMEM), anywhere],
        out_specs=[pl.BlockSpec(memory_space=pltpu.VMEM)] * len(cuts),
        out_shape=[jax.ShapeDtypeStruct((len(rels[0]), own, size), activations.dtype) for _, size in cuts],
        scratch_shapes=[pltpu.SemaphoreType.DMA((len(cuts), len(rels[0])))],
        compiler_params=pltpu.CompilerParams(vmem_limit_bytes=56 * megabyte),
        cost_estimate=pl.CostEstimate(flops=0, bytes_accessed=6 * 10**6, transcendentals=0),
        name="chosen",
    )(here, activations)


def partials(left, activations, depth, rels, cuts, paired):
    rank = left.shape[0]
    if not aligned(depth, [size for _, size in cuts]):
        outs = []
        for own, part, pair in zip(rels, cuts, paired):
            rows = taken(activations, depth, own, *part)
            term = jnp.einsum("kt,rtb->rkb", left, rows, preferred_element_type=jnp.float32)
            if pair is not None:
                term = term + jnp.einsum("kt,rtb->rkb", pair[0], pair[1], preferred_element_type=jnp.float32)
            outs.append(term.astype(jnp.bfloat16))
        return outs
    source = jnp.asarray(rels, jnp.int32) ^ lax.axis_index("dp")
    pairs = [pair for pair in paired if pair is not None]

    def kernel(source_ref, left_ref, block_ref, *refs):
        others = list(refs[: 2 * len(pairs)])
        for c, ((start, size), pair) in enumerate(zip(cuts, paired)):
            out_ref = refs[2 * len(pairs) + c]
            other_left_ref, other_ref = (others.pop(0), others.pop(0)) if pair is not None else (None, None)

            def one(i, carry):
                at = pl.multiple_of(source_ref[c, i] * depth + start, 128)
                term = jnp.dot(left_ref[...], block_ref[:, pl.ds(at, size)], preferred_element_type=jnp.float32)
                if other_ref is not None:
                    term = term + jnp.dot(other_left_ref[...], other_ref[i], preferred_element_type=jnp.float32)
                out_ref[i] = term.astype(out_ref.dtype)
                return carry

            lax.fori_loop(0, len(rels[c]), one, 0)

    vmem = pl.BlockSpec(memory_space=pltpu.VMEM)
    return pl.pallas_call(
        kernel,
        in_specs=[pl.BlockSpec(memory_space=pltpu.SMEM)] + [vmem] * (2 + 2 * len(pairs)),
        out_specs=[vmem] * len(cuts),
        out_shape=[jax.ShapeDtypeStruct((len(rels[0]), rank, size), jnp.bfloat16) for _, size in cuts],
        compiler_params=pltpu.CompilerParams(vmem_limit_bytes=24 * megabyte),
        cost_estimate=pl.CostEstimate(flops=10**9, bytes_accessed=5 * 10**6, transcendentals=0),
        name="partials",
    )(source, left, activations, *[value for pair in pairs for value in pair])


def finish(kept, arrived, tokens):
    rank = kept[0].shape[1]
    sizes = [value.shape[2] for value in kept]
    depth = sum(sizes)
    if not aligned(depth, sizes):
        columns = [a[0].astype(jnp.float32) + b[0].astype(jnp.float32) for a, b in zip(kept, arrived)]
        columns = jnp.concatenate(columns, axis=1) / tokens
        return columns.astype(jnp.bfloat16).T, mul(columns, columns, ((1,), (1,)))

    def kernel(*refs):
        rows_ref, moment_ref = refs[-2:]
        start, moment = 0, 0.0
        for c, size in enumerate(sizes):
            columns = (refs[c][0].astype(jnp.float32) + refs[len(sizes) + c][0].astype(jnp.float32)) * (1.0 / tokens)
            moment = moment + mul(columns, columns, ((1,), (1,)))
            rows_ref[start : start + size, :] = columns.T.astype(rows_ref.dtype)
            start += size
        moment_ref[...] = moment

    return pl.pallas_call(
        kernel,
        out_shape=[
            jax.ShapeDtypeStruct((depth, rank), jnp.bfloat16),
            jax.ShapeDtypeStruct((rank, rank), jnp.float32),
        ],
        compiler_params=pltpu.CompilerParams(vmem_limit_bytes=10 * megabyte),
        cost_estimate=pl.CostEstimate(flops=10**9, bytes_accessed=3 * 10**6, transcendentals=0),
        name="finish",
    )(*kept, *arrived)


def project(me, gradient, total, factors, rels, starts, depth):
    rank, width = factors[0].shape[2], gradient.shape[1]

    tallest = max(value.shape[0] * value.shape[1] for value in factors)

    def kernel(me_ref, total_ref, gradient_ref, *refs):
        ins, (out_ref, held, facing, sems) = refs[: len(factors)], refs[len(factors) :]

        def fetch(q):
            size = factors[q].shape[1]
            out = []
            for b, rel in enumerate(rels[q]):
                at = pl.multiple_of((me_ref[0] ^ rel) * depth + starts[q], 16)
                rows = pl.ds(b * size, size)
                out.append(pltpu.make_async_copy(ins[q].at[b], held.at[q % 3, rows], sems.at[q % 3, 2 * b]))
                source = gradient_ref.at[pl.ds(at, size)]
                out.append(pltpu.make_async_copy(source, facing.at[q % 3, rows], sems.at[q % 3, 2 * b + 1]))
            return out

        for q in range(min(2, len(factors))):
            for copy in fetch(q):
                copy.start()
        out_ref[...] = total_ref[...]
        for q, factor in enumerate(factors):
            for copy in fetch(q):
                copy.wait()
            if q + 2 < len(factors):
                for copy in fetch(q + 2):
                    copy.start()
            rows = slice(0, factor.shape[0] * factor.shape[1])
            out_ref[...] += low_mul(held[q % 3, rows, :], facing[q % 3, rows, :], ((0,), (0,)))

    return pl.pallas_call(
        kernel,
        in_specs=[pl.BlockSpec(memory_space=pltpu.SMEM), pl.BlockSpec(memory_space=pltpu.VMEM)]
        + [pl.BlockSpec(memory_space=pl.ANY)] * (1 + len(factors)),
        out_specs=pl.BlockSpec(memory_space=pltpu.VMEM),
        out_shape=jax.ShapeDtypeStruct((rank, width), jnp.float32),
        scratch_shapes=[
            pltpu.VMEM((3, tallest, rank), factors[0].dtype),
            pltpu.VMEM((3, tallest, width), gradient.dtype),
            pltpu.SemaphoreType.DMA((3, 2 * max(len(own) for own in rels))),
        ],
        compiler_params=pltpu.CompilerParams(vmem_limit_bytes=28 * megabyte),
        cost_estimate=pl.CostEstimate(flops=10**8, bytes_accessed=10**6, transcendentals=0),
        name="project",
    )(me, total, gradient, *factors)


def correct(me, solver, projected, gradient, factors, rels, cuts, part_of, depth):
    rank, width = projected[0].shape
    blocks = gradient.shape[0] // depth
    tile = max(t for t in range(16, min(depth, 512) + 1, 16) if depth % t == 0)
    found = {(part_of[q], rel): (q, b) for q in range(len(factors)) for b, rel in enumerate(rels[q])}

    def kernel(me_ref, solver_ref, *refs):
        projected_refs, (gradient_ref, *refs) = refs[: len(projected)], refs[len(projected) :]
        ins, (out_ref, weights_ref, held, facing, done, in_sems, out_sems) = refs[: len(factors)], refs[len(factors) :]

        def base(i):
            return pl.multiple_of((me_ref[0] ^ i) * depth, 16)

        def fetch(i):
            whole = gradient_ref.at[pl.ds(base(i), depth)]
            out = [pltpu.make_async_copy(whole, facing.at[i % 3], in_sems.at[i % 3, len(cuts)])]
            for c, (start, size) in enumerate(cuts):
                q, b = found[c, i]
                into = held.at[i % 3, pl.ds(start, size)]
                out.append(pltpu.make_async_copy(ins[q].at[b], into, in_sems.at[i % 3, c]))
            return out

        def store(i):
            return pltpu.make_async_copy(done.at[i % 2], out_ref.at[pl.ds(base(i), depth)], out_sems.at[i % 2])

        for i in range(min(2, blocks)):
            for copy in fetch(i):
                copy.start()
        total = projected_refs[0][...]
        for ref in projected_refs[1:]:
            total = total + ref[...]
        weights_ref[...] = mul(solver_ref[...], total).astype(weights_ref.dtype)
        for i in range(blocks):
            for copy in fetch(i):
                copy.wait()
            if i + 2 < blocks:
                for copy in fetch(i + 2):
                    copy.start()
            if i >= 2:
                store(i - 2).wait()

            def one(t, carry):
                rows = pl.ds(pl.multiple_of(t * tile, 16), tile)
                term = jnp.dot(held[i % 3, rows, :], weights_ref[...], preferred_element_type=jnp.float32)
                done[i % 2, rows, :] = (facing[i % 3, rows, :].astype(jnp.float32) - term).astype(done.dtype)
                return carry

            lax.fori_loop(0, depth // tile, one, 0)
            store(i).start()
        for i in range(max(0, blocks - 2), blocks):
            store(i).wait()

    vmem = pl.BlockSpec(memory_space=pltpu.VMEM)
    return pl.pallas_call(
        kernel,
        in_specs=[pl.BlockSpec(memory_space=pltpu.SMEM)]
        + [vmem] * (1 + len(projected))
        + [pl.BlockSpec(memory_space=pl.ANY)] * (1 + len(factors)),
        out_specs=pl.BlockSpec(memory_space=pl.ANY),
        out_shape=jax.ShapeDtypeStruct(gradient.shape, gradient.dtype),
        scratch_shapes=[
            pltpu.VMEM((rank, width), jnp.bfloat16),
            pltpu.VMEM((3, depth, rank), jnp.bfloat16),
            pltpu.VMEM((3, depth, width), gradient.dtype),
            pltpu.VMEM((2, depth, width), gradient.dtype),
            pltpu.SemaphoreType.DMA((3, len(cuts) + 1)),
            pltpu.SemaphoreType.DMA((2,)),
        ],
        compiler_params=pltpu.CompilerParams(vmem_limit_bytes=32 * megabyte),
        cost_estimate=pl.CostEstimate(flops=7 * 10**9, bytes_accessed=70 * 10**6, transcendentals=0),
        name="correct",
    )(me, solver, *projected, gradient, *factors)


def cut(extent, shares):
    unit = extent // sum(shares)
    out, start = [], 0
    for i, share in enumerate(shares):
        size = unit * share if i + 1 < len(shares) else extent - start
        out.append((start, size))
        start += size
    return out


def split_pairs(values, groups=2):
    size = len(values) // groups
    return [list(values[i * size : (i + 1) * size]) for i in range(groups)]


def local(activations, test_matrix, gradient):
    count = lax.axis_size("dp")
    me = lax.axis_index("dp")
    own, hidden = activations.shape
    tokens = own * count
    probes = test_matrix.shape[1]
    rank = probes * count
    depth = hidden // count
    bx, by, bl = 1, 2, 4
    lead = [1 << i for i in range(3, count.bit_length() - 1)][::-1]
    every = list(range(count))
    rotations = ((bx, by, bl), (by, bl, bx), (bl, bx, by))

    parts = cut(depth, (4, 4, 3, 1, 1))
    orders = [
        lead + [bl, by],
        lead + [bx, bl],
        lead + [bl, by, bx],
        [by, bx] + lead + [bl],
        lead + [bl, bx, by],
    ]
    swaps = (bx, by)

    probe_rows = test_matrix.T
    give = chosen(activations, depth, [[r | bit for r in places(order)] for order, bit in zip(orders, swaps)], parts[:2])
    swapped = [across(value, bit) for value, bit in zip(give, swaps)]
    for bit in lead:
        probe_rows = jnp.concatenate([probe_rows, across(probe_rows, bit)], axis=0)
    probe_rows, *swapped = round_end(probe_rows, *swapped)
    strips = cut(hidden, (69, 69, 70))
    first = [probe_rows[:, start : start + size] for start, size in strips]
    arrived = [across(value, order[0]) for value, order in zip(first, rotations)]
    first = [jnp.concatenate(pair, axis=0) for pair in zip(first, arrived)]
    first = round_end(*first)
    second = [across(value, order[1]) for value, order in zip(first, rotations)]
    first, second = split_pairs(round_end(*first, *second))

    def sketch_of(strip, rows):
        start, size = strip
        return low_mul(activations[:, start : start + size], rows, ((1,), (1,)))

    third = [across(value, order[2]) for value, order in zip(first, rotations)]
    terms = [[sketch_of(strip, jnp.concatenate(pair, axis=0))] for strip, pair in zip(strips, zip(first, second))]
    ended = round_end(*third, *second, *[value for term in terms for value in term])
    third, second, terms = split_pairs(ended, 3)
    terms = [[value] for value in terms]
    fourth = [across(value, order[2]) for value, order in zip(second, rotations)]
    for term, strip, value in zip(terms, strips, third):
        term.append(sketch_of(strip, value))
    fourth = round_end(*fourth, *[value for term in terms for value in term])[: len(strips)]
    for term, strip, value in zip(terms, strips, fourth):
        term.append(sketch_of(strip, value))
    spread = []
    for order in rotations:
        source = jnp.asarray(places(lead + list(order)), jnp.int32) ^ me
        columns = jnp.repeat(source, probes) * probes + jnp.tile(jnp.arange(probes), count)
        spread.append((columns[:, None] == jnp.arange(rank)).astype(jnp.float32))
    terms = [value for term in terms for value in term]
    sketch = total_tensor(mul(jnp.concatenate(terms, axis=1), jnp.concatenate(spread, axis=0)))
    sketch_low = sketch.astype(jnp.bfloat16)
    left = sketch_low.T

    steps = [list(reversed(order)) for order in orders]
    rels = [places(order) for order in orders]
    half = [len(order) // 2 for order in rels]
    pairs = [None] * len(parts)
    sent, kept = [None] * len(parts), [None] * len(parts)
    for c in range(2, len(parts)):
        (sent[c],) = partials(left, activations, depth, [rels[c][half[c] :]], [parts[c]], [None])
    other_left = [across(left, bit) for bit in swaps]
    *other_left, sent[2] = round_end(*other_left, sent[2])
    for c in range(2):
        pair = (other_left[c], swapped[c])
        (sent[c],) = partials(
            left, activations, depth, [rels[c][half[c] :]], [parts[c]], [(pair[0], pair[1][half[c] :])]
        )
        pairs[c] = (pair[0], pair[1][: half[c]])
    left, sent[0], sent[1] = round_end(left, sent[0], sent[1])
    kept[2:] = partials(
        left, activations, depth, [rels[c][: half[c]] for c in range(2, len(parts))], parts[2:], pairs[2:]
    )
    kept[:2] = partials(left, activations, depth, [rels[c][: half[c]] for c in range(2)], parts[:2], pairs[:2])
    core = mul(sketch, sketch_low.astype(jnp.float32), ((0,), (0,)))
    core = my_half(core) if two_cores() else core
    turn = 0
    while True:
        arrived = [across(sent[c], step[0]) if step else None for c, step in enumerate(steps)]
        for bit in (lead, [], [bx, by], [bl], [])[min(turn, 4)]:
            core = core + across(core, bit)
        turn += 1
        for c, step in enumerate(steps):
            if len(step) > 1:
                cutting = kept[c].shape[0] // 2
                total = [
                    kept[c][rows].astype(jnp.float32) + arrived[c][rows].astype(jnp.float32)
                    for rows in (slice(cutting, None), slice(0, cutting))
                ]
                sent[c], kept[c] = [value.astype(jnp.bfloat16) for value in total]
                step.pop(0)
            elif step:
                sent[c] = arrived[c]
                step.pop(0)
        *ended, core = round_end(*sent, *kept, core)
        sent, kept = split_pairs(ended)
        if not any(steps):
            break
    rows, moment = finish(kept, sent, tokens)
    core = (both_halves(core) if two_cores() else core) / tokens
    core = 0.5 * (core + core.T)

    rows = rows[None]
    for bit in lead:
        rows = jnp.concatenate([rows, across(rows, bit)], axis=0)
    if two_cores():
        moment = my_half(moment) + other_core(my_half(moment, other=True))
    for bit in [bx, by, bl]:
        moment = moment + across(moment, bit)
    inverse = lower_inverse(core)
    rows, moment, inverse = round_end(rows, moment, inverse)
    third = 16 * round(depth / 48)
    shares = [(0, third), (third, third), (2 * third, depth - 2 * third)]
    first = [rows[:, start : start + size] for start, size in shares]
    arrived = [across(value, order[0]) for value, order in zip(first, rotations)]
    for bit in lead:
        moment = moment + across(moment, bit)
    moment = both_halves(moment) if two_cores() else lax.psum(moment, "tensor")
    first = [jnp.concatenate(pair, axis=0) for pair in zip(first, arrived)]
    first = round_end(*first)
    second = [across(value, order[1]) for value, order in zip(first, rotations)]
    gram = mul(mul(inverse, moment), inverse, ((1,), (1,)))
    damping = damping_ratio * jnp.trace(gram) / rank
    last = lower_inverse(gram + damping * jnp.eye(rank, dtype=jnp.float32))
    *both, gram, last = round_end(*first, *second, gram, last)
    first, second = split_pairs(both)
    starts = [start for start, _ in shares]
    near = [places(lead + [order[0]]) for order in rotations]
    next_to = [[r ^ order[1] for r in rs] for rs, order in zip(near, rotations)]
    far = [[r ^ order[2] for r in rs] for rs, order in zip(near, rotations)]
    farthest = [[r ^ order[2] for r in rs] for rs, order in zip(next_to, rotations)]
    here = me[None]
    third = [across(value, order[2]) for value, order in zip(first, rotations)]
    step = mul(last, inverse)
    solver = mul(step, step, ((0,), (0,)))
    projected = jnp.zeros((rank, gradient.shape[1]), jnp.float32)
    projected = project(here, gradient, projected, first + second, near + next_to, starts * 2, depth)
    *ended, solver, projected = round_end(*third, *second, solver, projected)
    third, second = split_pairs(ended)
    fourth = [across(value, order[2]) for value, order in zip(second, rotations)]
    projected = project(here, gradient, projected, third, far, starts, depth)
    *fourth, projected = round_end(*fourth, projected)
    projected = project(here, gradient, projected, fourth, farthest, starts, depth)
    projected = (projected, other_core(projected)) if two_cores() else (lax.psum(projected, "tensor"),)
    out = correct(
        here,
        solver,
        projected,
        gradient,
        first + second + third + fourth,
        near + next_to + far + farthest,
        shares,
        [0, 1, 2] * 4,
        depth,
    )
    return out, gram


def solution(mesh):
    placed = (P("dp", "tensor"), P("tensor", "dp"), P("tensor", "dp"))
    return jax.shard_map(
        local, mesh=mesh, in_specs=placed, out_specs=(P("tensor", "dp"), P()), check_vma=False
    )
```

```python
import jax
import jax.numpy as jnp
from jax import lax
from jax.experimental import pallas as pl
from jax.experimental.pallas import tpu as pltpu
from jax.sharding import PartitionSpec as P

damping_ratio = 0.1
exact = lax.Precision.HIGHEST
megabyte = 1024 * 1024


def mul(a, b, dims=((1,), (0,))):
    return lax.dot_general(a, b, (dims, ((), ())), precision=exact, preferred_element_type=jnp.float32)


def low_mul(a, b, dims=((1,), (0,))):
    return lax.dot_general(a, b, (dims, ((), ())), preferred_element_type=jnp.float32)


def across(value, bit):
    count = lax.axis_size("dp")
    return lax.ppermute(value, "dp", [(i, i ^ bit) for i in range(count)])


def total_tensor(value):
    return value + other_core(value) if two_cores() else lax.psum(value, "tensor")


def two_cores():
    return lax.axis_size("tensor") == 2


def my_half(value, other=False):
    half = value.shape[0] // 2
    core = lax.axis_index("tensor")
    return lax.dynamic_slice_in_dim(value, (1 - core if other else core) * half, half, axis=0)


def other_core(value):
    return lax.ppermute(value, "tensor", [(0, 1), (1, 0)])


def both_halves(mine):
    theirs = other_core(mine)
    first = lax.axis_index("tensor") == 0
    return jnp.concatenate([jnp.where(first, mine, theirs), jnp.where(first, theirs, mine)], axis=0)


def round_end(*values):
    return lax.optimization_barrier(values)


def places(bits):
    found = [0]
    for bit in bits:
        found = found + [i ^ bit for i in found]
    return found


def small_inverse(block):
    side = block.shape[0]
    lanes = lax.broadcasted_iota(jnp.int32, (side, side), 1)
    eye = (lax.broadcasted_iota(jnp.int32, (side, side), 0) == lanes).astype(jnp.float32)
    full = jnp.concatenate([block, eye], axis=1)
    work = [full[g : g + 8] for g in range(0, side, 8)]
    pivots = [jnp.ones((8, 1), jnp.float32) for _ in work]
    rows = lax.broadcasted_iota(jnp.int32, (8, 1), 0)
    for j in range(side):
        own, r = divmod(j, 8)
        row = work[own][r : r + 1, :]
        pivot = row[:, j : j + 1]
        pivots[own] = jnp.where(rows == r, pivot, pivots[own])
        unit = row * (1.0 / pivot)
        if r < 7:
            work[own] = work[own] - jnp.where(rows > r, work[own][:, j : j + 1], 0.0) * unit
        for g in range(own + 1, len(work)):
            work[g] = work[g] - work[g][:, j : j + 1] * unit
    return jnp.concatenate([w[:, side:] * lax.rsqrt(p) for w, p in zip(work, pivots)], axis=0)


def lower_inverse_kernel(matrix_ref, out_ref, left_ref):
    size = matrix_ref.shape[0]
    side = min(128, size)
    out_ref[...] = jnp.zeros(out_ref.shape, jnp.float32)
    left_ref[...] = matrix_ref[...]
    for k in range(0, size, side):
        own = pl.ds(k, side)
        block = small_inverse(left_ref[own, k : k + side])
        if k:
            out_ref[own, :k] = -mul(block, mul(left_ref[own, :k], out_ref[:k, :k]))
        out_ref[own, k : k + side] = block
        if k + side < size:
            rest = pl.ds(k + side, size - k - side)
            lower = mul(left_ref[rest, k : k + side], block, ((1,), (1,)))
            left_ref[rest, k : k + side] = lower
            left_ref[rest, k + side :] = left_ref[rest, k + side :] - mul(lower, lower, ((1,), (1,)))


def lower_inverse(matrix):
    return pl.pallas_call(
        lower_inverse_kernel,
        out_shape=jax.ShapeDtypeStruct(matrix.shape, jnp.float32),
        scratch_shapes=[pltpu.VMEM(matrix.shape, jnp.float32)],
        compiler_params=pltpu.CompilerParams(vmem_limit_bytes=12 * megabyte),
        cost_estimate=pl.CostEstimate(flops=10**8, bytes_accessed=10**6, transcendentals=0),
        name="lower_inverse",
    )(matrix)


def aligned(depth, sizes):
    return depth % 128 == 0 and all(size % 128 == 0 for size in sizes)


def taken(activations, depth, rels, start, size):
    blocks = activations.reshape(activations.shape[0], -1, depth)[:, :, start : start + size]
    return jnp.take(blocks, jnp.asarray(rels, jnp.int32) ^ lax.axis_index("dp"), axis=1).transpose(1, 0, 2)


def chosen(activations, depth, rels, cuts):
    if not aligned(depth, [size for _, size in cuts]):
        return [taken(activations, depth, own, *part) for own, part in zip(rels, cuts)]
    own = activations.shape[0]
    here = lax.axis_index("dp")[None]

    def kernel(here_ref, in_ref, *refs):
        out_refs, sems = refs[:-1], refs[-1]
        copies = []
        for c, (start, size) in enumerate(cuts):
            for i, rel in enumerate(rels[c]):
                at = pl.multiple_of((here_ref[0] ^ rel) * depth + start, 128)
                source = in_ref.at[:, pl.ds(at, size)]
                copies.append(pltpu.make_async_copy(source, out_refs[c].at[i], sems.at[c, i]))
        for copy in copies:
            copy.start()
        for copy in copies:
            copy.wait()

    anywhere = pl.BlockSpec(memory_space=pl.ANY)
    return pl.pallas_call(
        kernel,
        in_specs=[pl.BlockSpec(memory_space=pltpu.SMEM), anywhere],
        out_specs=[pl.BlockSpec(memory_space=pltpu.VMEM)] * len(cuts),
        out_shape=[jax.ShapeDtypeStruct((len(rels[0]), own, size), activations.dtype) for _, size in cuts],
        scratch_shapes=[pltpu.SemaphoreType.DMA((len(cuts), len(rels[0])))],
        compiler_params=pltpu.CompilerParams(vmem_limit_bytes=56 * megabyte),
        cost_estimate=pl.CostEstimate(flops=0, bytes_accessed=6 * 10**6, transcendentals=0),
        name="chosen",
    )(here, activations)


def partials(left, activations, depth, rels, cuts, paired):
    rank = left.shape[0]
    if not aligned(depth, [size for _, size in cuts]):
        outs = []
        for own, part, pair in zip(rels, cuts, paired):
            rows = taken(activations, depth, own, *part)
            term = jnp.einsum("kt,rtb->rkb", left, rows, preferred_element_type=jnp.float32)
            if pair is not None:
                term = term + jnp.einsum("kt,rtb->rkb", pair[0], pair[1], preferred_element_type=jnp.float32)
            outs.append(term.astype(jnp.bfloat16))
        return outs
    source = jnp.asarray(rels, jnp.int32) ^ lax.axis_index("dp")
    pairs = [pair for pair in paired if pair is not None]

    def kernel(source_ref, left_ref, block_ref, *refs):
        others = list(refs[: 2 * len(pairs)])
        for c, ((start, size), pair) in enumerate(zip(cuts, paired)):
            out_ref = refs[2 * len(pairs) + c]
            other_left_ref, other_ref = (others.pop(0), others.pop(0)) if pair is not None else (None, None)

            def one(i, carry):
                at = pl.multiple_of(source_ref[c, i] * depth + start, 128)
                term = jnp.dot(left_ref[...], block_ref[:, pl.ds(at, size)], preferred_element_type=jnp.float32)
                if other_ref is not None:
                    term = term + jnp.dot(other_left_ref[...], other_ref[i], preferred_element_type=jnp.float32)
                out_ref[i] = term.astype(out_ref.dtype)
                return carry

            lax.fori_loop(0, len(rels[c]), one, 0)

    vmem = pl.BlockSpec(memory_space=pltpu.VMEM)
    return pl.pallas_call(
        kernel,
        in_specs=[pl.BlockSpec(memory_space=pltpu.SMEM)] + [vmem] * (2 + 2 * len(pairs)),
        out_specs=[vmem] * len(cuts),
        out_shape=[jax.ShapeDtypeStruct((len(rels[0]), rank, size), jnp.bfloat16) for _, size in cuts],
        compiler_params=pltpu.CompilerParams(vmem_limit_bytes=24 * megabyte),
        cost_estimate=pl.CostEstimate(flops=10**9, bytes_accessed=5 * 10**6, transcendentals=0),
        name="partials",
    )(source, left, activations, *[value for pair in pairs for value in pair])


def finish(kept, arrived, tokens):
    rank = kept[0].shape[1]
    sizes = [value.shape[2] for value in kept]
    depth = sum(sizes)
    if not aligned(depth, sizes):
        columns = [a[0].astype(jnp.float32) + b[0].astype(jnp.float32) for a, b in zip(kept, arrived)]
        columns = jnp.concatenate(columns, axis=1) / tokens
        return columns.astype(jnp.bfloat16).T, mul(columns, columns, ((1,), (1,)))

    def kernel(*refs):
        rows_ref, moment_ref = refs[-2:]
        start, moment = 0, 0.0
        for c, size in enumerate(sizes):
            columns = (refs[c][0].astype(jnp.float32) + refs[len(sizes) + c][0].astype(jnp.float32)) * (1.0 / tokens)
            moment = moment + mul(columns, columns, ((1,), (1,)))
            rows_ref[start : start + size, :] = columns.T.astype(rows_ref.dtype)
            start += size
        moment_ref[...] = moment

    return pl.pallas_call(
        kernel,
        out_shape=[
            jax.ShapeDtypeStruct((depth, rank), jnp.bfloat16),
            jax.ShapeDtypeStruct((rank, rank), jnp.float32),
        ],
        compiler_params=pltpu.CompilerParams(vmem_limit_bytes=10 * megabyte),
        cost_estimate=pl.CostEstimate(flops=10**9, bytes_accessed=3 * 10**6, transcendentals=0),
        name="finish",
    )(*kept, *arrived)


def project(me, gradient, total, factors, rels, starts, depth):
    rank, width = factors[0].shape[2], gradient.shape[1]

    tallest = max(value.shape[0] * value.shape[1] for value in factors)

    def kernel(me_ref, total_ref, gradient_ref, *refs):
        ins, (out_ref, held, facing, sems) = refs[: len(factors)], refs[len(factors) :]

        def fetch(q):
            size = factors[q].shape[1]
            out = []
            for b, rel in enumerate(rels[q]):
                at = pl.multiple_of((me_ref[0] ^ rel) * depth + starts[q], 16)
                rows = pl.ds(b * size, size)
                out.append(pltpu.make_async_copy(ins[q].at[b], held.at[q % 3, rows], sems.at[q % 3, 2 * b]))
                source = gradient_ref.at[pl.ds(at, size)]
                out.append(pltpu.make_async_copy(source, facing.at[q % 3, rows], sems.at[q % 3, 2 * b + 1]))
            return out

        for q in range(min(2, len(factors))):
            for copy in fetch(q):
                copy.start()
        out_ref[...] = total_ref[...]
        for q, factor in enumerate(factors):
            for copy in fetch(q):
                copy.wait()
            if q + 2 < len(factors):
                for copy in fetch(q + 2):
                    copy.start()
            rows = slice(0, factor.shape[0] * factor.shape[1])
            out_ref[...] += low_mul(held[q % 3, rows, :], facing[q % 3, rows, :], ((0,), (0,)))

    return pl.pallas_call(
        kernel,
        in_specs=[pl.BlockSpec(memory_space=pltpu.SMEM), pl.BlockSpec(memory_space=pltpu.VMEM)]
        + [pl.BlockSpec(memory_space=pl.ANY)] * (1 + len(factors)),
        out_specs=pl.BlockSpec(memory_space=pltpu.VMEM),
        out_shape=jax.ShapeDtypeStruct((rank, width), jnp.float32),
        scratch_shapes=[
            pltpu.VMEM((3, tallest, rank), factors[0].dtype),
            pltpu.VMEM((3, tallest, width), gradient.dtype),
            pltpu.SemaphoreType.DMA((3, 2 * max(len(own) for own in rels))),
        ],
        compiler_params=pltpu.CompilerParams(vmem_limit_bytes=28 * megabyte),
        cost_estimate=pl.CostEstimate(flops=10**8, bytes_accessed=10**6, transcendentals=0),
        name="project",
    )(me, total, gradient, *factors)


def correct(me, solver, projected, gradient, factors, rels, cuts, part_of, depth):
    rank, width = projected[0].shape
    blocks = gradient.shape[0] // depth
    tile = max(t for t in range(16, min(depth, 512) + 1, 16) if depth % t == 0)
    found = {(part_of[q], rel): (q, b) for q in range(len(factors)) for b, rel in enumerate(rels[q])}

    def kernel(me_ref, solver_ref, *refs):
        projected_refs, (gradient_ref, *refs) = refs[: len(projected)], refs[len(projected) :]
        ins, (out_ref, weights_ref, held, facing, done, in_sems, out_sems) = refs[: len(factors)], refs[len(factors) :]

        def base(i):
            return pl.multiple_of((me_ref[0] ^ i) * depth, 16)

        def fetch(i):
            whole = gradient_ref.at[pl.ds(base(i), depth)]
            out = [pltpu.make_async_copy(whole, facing.at[i % 3], in_sems.at[i % 3, len(cuts)])]
            for c, (start, size) in enumerate(cuts):
                q, b = found[c, i]
                into = held.at[i % 3, pl.ds(start, size)]
                out.append(pltpu.make_async_copy(ins[q].at[b], into, in_sems.at[i % 3, c]))
            return out

        def store(i):
            return pltpu.make_async_copy(done.at[i % 2], out_ref.at[pl.ds(base(i), depth)], out_sems.at[i % 2])

        for i in range(min(2, blocks)):
            for copy in fetch(i):
                copy.start()
        total = projected_refs[0][...]
        for ref in projected_refs[1:]:
            total = total + ref[...]
        weights_ref[...] = mul(solver_ref[...], total).astype(weights_ref.dtype)
        for i in range(blocks):
            for copy in fetch(i):
                copy.wait()
            if i + 2 < blocks:
                for copy in fetch(i + 2):
                    copy.start()
            if i >= 2:
                store(i - 2).wait()

            def one(t, carry):
                rows = pl.ds(pl.multiple_of(t * tile, 16), tile)
                term = jnp.dot(held[i % 3, rows, :], weights_ref[...], preferred_element_type=jnp.float32)
                done[i % 2, rows, :] = (facing[i % 3, rows, :].astype(jnp.float32) - term).astype(done.dtype)
                return carry

            lax.fori_loop(0, depth // tile, one, 0)
            store(i).start()
        for i in range(max(0, blocks - 2), blocks):
            store(i).wait()

    vmem = pl.BlockSpec(memory_space=pltpu.VMEM)
    return pl.pallas_call(
        kernel,
        in_specs=[pl.BlockSpec(memory_space=pltpu.SMEM)]
        + [vmem] * (1 + len(projected))
        + [pl.BlockSpec(memory_space=pl.ANY)] * (1 + len(factors)),
        out_specs=pl.BlockSpec(memory_space=pl.ANY),
        out_shape=jax.ShapeDtypeStruct(gradient.shape, gradient.dtype),
        scratch_shapes=[
            pltpu.VMEM((rank, width), jnp.bfloat16),
            pltpu.VMEM((3, depth, rank), jnp.bfloat16),
            pltpu.VMEM((3, depth, width), gradient.dtype),
            pltpu.VMEM((2, depth, width), gradient.dtype),
            pltpu.SemaphoreType.DMA((3, len(cuts) + 1)),
            pltpu.SemaphoreType.DMA((2,)),
        ],
        compiler_params=pltpu.CompilerParams(vmem_limit_bytes=32 * megabyte),
        cost_estimate=pl.CostEstimate(flops=7 * 10**9, bytes_accessed=70 * 10**6, transcendentals=0),
        name="correct",
    )(me, solver, *projected, gradient, *factors)


def cut(extent, shares):
    unit = extent // sum(shares)
    out, start = [], 0
    for i, share in enumerate(shares):
        size = unit * share if i + 1 < len(shares) else extent - start
        out.append((start, size))
        start += size
    return out


def split_pairs(values, groups=2):
    size = len(values) // groups
    return [list(values[i * size : (i + 1) * size]) for i in range(groups)]


def local(activations, test_matrix, gradient):
    count = lax.axis_size("dp")
    me = lax.axis_index("dp")
    own, hidden = activations.shape
    tokens = own * count
    probes = test_matrix.shape[1]
    rank = probes * count
    depth = hidden // count
    bx, by, bl = 1, 2, 4
    lead = [1 << i for i in range(3, count.bit_length() - 1)][::-1]
    every = list(range(count))
    rotations = ((bx, by, bl), (by, bl, bx), (bl, bx, by))

    parts = cut(depth, (4, 4, 3, 1, 1))
    orders = [
        lead + [bl, by],
        lead + [bx, bl],
        lead + [bl, by, bx],
        [by, bx] + lead + [bl],
        lead + [bl, bx, by],
    ]
    swaps = (bx, by)

    probe_rows = test_matrix.T
    give = chosen(activations, depth, [[r | bit for r in places(order)] for order, bit in zip(orders, swaps)], parts[:2])
    swapped = [across(value, bit) for value, bit in zip(give, swaps)]
    for bit in lead:
        probe_rows = jnp.concatenate([probe_rows, across(probe_rows, bit)], axis=0)
    probe_rows, *swapped = round_end(probe_rows, *swapped)
    strips = cut(hidden, (69, 69, 70))
    first = [probe_rows[:, start : start + size] for start, size in strips]
    arrived = [across(value, order[0]) for value, order in zip(first, rotations)]
    first = [jnp.concatenate(pair, axis=0) for pair in zip(first, arrived)]
    first = round_end(*first)
    second = [across(value, order[1]) for value, order in zip(first, rotations)]
    first, second = split_pairs(round_end(*first, *second))

    def sketch_of(strip, rows):
        start, size = strip
        return low_mul(activations[:, start : start + size], rows, ((1,), (1,)))

    third = [across(value, order[2]) for value, order in zip(first, rotations)]
    terms = [[sketch_of(strip, jnp.concatenate(pair, axis=0))] for strip, pair in zip(strips, zip(first, second))]
    ended = round_end(*third, *second, *[value for term in terms for value in term])
    third, second, terms = split_pairs(ended, 3)
    terms = [[value] for value in terms]
    fourth = [across(value, order[2]) for value, order in zip(second, rotations)]
    for term, strip, value in zip(terms, strips, third):
        term.append(sketch_of(strip, value))
    fourth = round_end(*fourth, *[value for term in terms for value in term])[: len(strips)]
    for term, strip, value in zip(terms, strips, fourth):
        term.append(sketch_of(strip, value))
    spread = []
    for order in rotations:
        source = jnp.asarray(places(lead + list(order)), jnp.int32) ^ me
        columns = jnp.repeat(source, probes) * probes + jnp.tile(jnp.arange(probes), count)
        spread.append((columns[:, None] == jnp.arange(rank)).astype(jnp.float32))
    terms = [value for term in terms for value in term]
    sketch = total_tensor(mul(jnp.concatenate(terms, axis=1), jnp.concatenate(spread, axis=0)))
    sketch_low = sketch.astype(jnp.bfloat16)
    left = sketch_low.T

    steps = [list(reversed(order)) for order in orders]
    rels = [places(order) for order in orders]
    half = [len(order) // 2 for order in rels]
    pairs = [None] * len(parts)
    sent, kept = [None] * len(parts), [None] * len(parts)
    other_left = [across(left, bit) for bit in swaps]
    (sent[2],) = partials(left, activations, depth, [rels[2][half[2] :]], parts[2:3], [None])
    other_left = round_end(*other_left, sent[2])[:2]
    for c in range(2):
        pairs[c] = (other_left[c], swapped[c][half[c] :])
    sent[:2] = partials(left, activations, depth, [rels[c][half[c] :] for c in range(2)], parts[:2], pairs[:2])
    left = round_end(left, *sent[:2])[0]
    sent[3:] = partials(
        left, activations, depth, [rels[c][half[c] :] for c in range(3, len(parts))], parts[3:], pairs[3:]
    )
    left = round_end(left, *sent[3:])[0]
    for c in range(2):
        pairs[c] = (other_left[c], swapped[c][: half[c]])
    kept[2:] = partials(
        left, activations, depth, [rels[c][: half[c]] for c in range(2, len(parts))], parts[2:], pairs[2:]
    )
    kept[:2] = partials(left, activations, depth, [rels[c][: half[c]] for c in range(2)], parts[:2], pairs[:2])
    core = mul(sketch, sketch_low.astype(jnp.float32), ((0,), (0,)))
    core = my_half(core) if two_cores() else core
    turn = 0
    while True:
        arrived = [across(sent[c], step[0]) if step else None for c, step in enumerate(steps)]
        if turn == 0:
            core, arrived[-1] = round_end(core, arrived[-1])
        for bit in (lead, [], [bx, by], [bl], [])[min(turn, 4)]:
            core = core + across(core, bit)
        turn += 1
        for c, step in enumerate(steps):
            if len(step) > 1:
                cutting = kept[c].shape[0] // 2
                total = [
                    kept[c][rows].astype(jnp.float32) + arrived[c][rows].astype(jnp.float32)
                    for rows in (slice(cutting, None), slice(0, cutting))
                ]
                sent[c], kept[c] = [value.astype(jnp.bfloat16) for value in total]
                step.pop(0)
            elif step:
                sent[c] = arrived[c]
                step.pop(0)
        *ended, core = round_end(*sent, *kept, core)
        sent, kept = split_pairs(ended)
        if not any(steps):
            break
    rows, moment = finish(kept, sent, tokens)
    core = (both_halves(core) if two_cores() else core) / tokens
    core = 0.5 * (core + core.T)

    rows = rows[None]
    for bit in lead:
        rows = jnp.concatenate([rows, across(rows, bit)], axis=0)
    if two_cores():
        moment = my_half(moment) + other_core(my_half(moment, other=True))
    for bit in [bx, by, bl]:
        moment = moment + across(moment, bit)
    inverse = lower_inverse(core)
    rows, moment, inverse = round_end(rows, moment, inverse)
    third = 16 * round(depth / 48)
    shares = [(0, third), (third, third), (2 * third, depth - 2 * third)]
    first = [rows[:, start : start + size] for start, size in shares]
    arrived = [across(value, order[0]) for value, order in zip(first, rotations)]
    for bit in lead:
        moment = moment + across(moment, bit)
    moment = both_halves(moment) if two_cores() else lax.psum(moment, "tensor")
    first = [jnp.concatenate(pair, axis=0) for pair in zip(first, arrived)]
    first = round_end(*first)
    second = [across(value, order[1]) for value, order in zip(first, rotations)]
    gram = mul(mul(inverse, moment), inverse, ((1,), (1,)))
    damping = damping_ratio * jnp.trace(gram) / rank
    last = lower_inverse(gram + damping * jnp.eye(rank, dtype=jnp.float32))
    *both, gram, last = round_end(*first, *second, gram, last)
    first, second = split_pairs(both)
    starts = [start for start, _ in shares]
    near = [places(lead + [order[0]]) for order in rotations]
    next_to = [[r ^ order[1] for r in rs] for rs, order in zip(near, rotations)]
    far = [[r ^ order[2] for r in rs] for rs, order in zip(near, rotations)]
    farthest = [[r ^ order[2] for r in rs] for rs, order in zip(next_to, rotations)]
    here = me[None]
    third = [across(value, order[2]) for value, order in zip(first, rotations)]
    step = mul(last, inverse)
    solver = mul(step, step, ((0,), (0,)))
    projected = jnp.zeros((rank, gradient.shape[1]), jnp.float32)
    projected = project(here, gradient, projected, first + second, near + next_to, starts * 2, depth)
    *ended, solver, projected = round_end(*third, *second, solver, projected)
    third, second = split_pairs(ended)
    fourth = [across(value, order[2]) for value, order in zip(second, rotations)]
    projected = project(here, gradient, projected, third, far, starts, depth)
    *fourth, projected = round_end(*fourth, projected)
    projected = project(here, gradient, projected, fourth, farthest, starts, depth)
    projected = (projected, other_core(projected)) if two_cores() else (lax.psum(projected, "tensor"),)
    out = correct(
        here,
        solver,
        projected,
        gradient,
        first + second + third + fourth,
        near + next_to + far + farthest,
        shares,
        [0, 1, 2] * 4,
        depth,
    )
    return out, gram


def solution(mesh):
    placed = (P("dp", "tensor"), P("tensor", "dp"), P("tensor", "dp"))
    return jax.shard_map(
        local, mesh=mesh, in_specs=placed, out_specs=(P("tensor", "dp"), P()), check_vma=False
    )
```

```python
import jax
import jax.numpy as jnp
from jax import lax
from jax.experimental import pallas as pl
from jax.experimental.pallas import tpu as pltpu
from jax.sharding import PartitionSpec as P

damping_ratio = 0.1
exact = lax.Precision.HIGHEST
megabyte = 1024 * 1024


def mul(a, b, dims=((1,), (0,))):
    return lax.dot_general(a, b, (dims, ((), ())), precision=exact, preferred_element_type=jnp.float32)


def low_mul(a, b, dims=((1,), (0,))):
    return lax.dot_general(a, b, (dims, ((), ())), preferred_element_type=jnp.float32)


def across(value, bit):
    count = lax.axis_size("dp")
    return lax.ppermute(value, "dp", [(i, i ^ bit) for i in range(count)])


def total_tensor(value):
    return value + other_core(value) if two_cores() else lax.psum(value, "tensor")


def two_cores():
    return lax.axis_size("tensor") == 2


def my_half(value, other=False):
    half = value.shape[0] // 2
    core = lax.axis_index("tensor")
    return lax.dynamic_slice_in_dim(value, (1 - core if other else core) * half, half, axis=0)


def other_core(value):
    return lax.ppermute(value, "tensor", [(0, 1), (1, 0)])


def both_halves(mine):
    theirs = other_core(mine)
    first = lax.axis_index("tensor") == 0
    return jnp.concatenate([jnp.where(first, mine, theirs), jnp.where(first, theirs, mine)], axis=0)


def round_end(*values):
    return lax.optimization_barrier(values)


def places(bits):
    found = [0]
    for bit in bits:
        found = found + [i ^ bit for i in found]
    return found


def small_inverse(block):
    side = block.shape[0]
    lanes = lax.broadcasted_iota(jnp.int32, (side, side), 1)
    eye = (lax.broadcasted_iota(jnp.int32, (side, side), 0) == lanes).astype(jnp.float32)
    full = jnp.concatenate([block, eye], axis=1)
    work = [full[g : g + 8] for g in range(0, side, 8)]
    pivots = [jnp.ones((8, 1), jnp.float32) for _ in work]
    rows = lax.broadcasted_iota(jnp.int32, (8, 1), 0)
    for j in range(side):
        own, r = divmod(j, 8)
        row = work[own][r : r + 1, :]
        pivot = row[:, j : j + 1]
        pivots[own] = jnp.where(rows == r, pivot, pivots[own])
        unit = row * (1.0 / pivot)
        if r < 7:
            work[own] = work[own] - jnp.where(rows > r, work[own][:, j : j + 1], 0.0) * unit
        for g in range(own + 1, len(work)):
            work[g] = work[g] - work[g][:, j : j + 1] * unit
    return jnp.concatenate([w[:, side:] * lax.rsqrt(p) for w, p in zip(work, pivots)], axis=0)


def lower_inverse_kernel(matrix_ref, out_ref, left_ref):
    size = matrix_ref.shape[0]
    side = min(128, size)
    out_ref[...] = jnp.zeros(out_ref.shape, jnp.float32)
    left_ref[...] = matrix_ref[...]
    for k in range(0, size, side):
        own = pl.ds(k, side)
        block = small_inverse(left_ref[own, k : k + side])
        if k:
            out_ref[own, :k] = -mul(block, mul(left_ref[own, :k], out_ref[:k, :k]))
        out_ref[own, k : k + side] = block
        if k + side < size:
            rest = pl.ds(k + side, size - k - side)
            lower = mul(left_ref[rest, k : k + side], block, ((1,), (1,)))
            left_ref[rest, k : k + side] = lower
            left_ref[rest, k + side :] = left_ref[rest, k + side :] - mul(lower, lower, ((1,), (1,)))


def lower_inverse(matrix):
    return pl.pallas_call(
        lower_inverse_kernel,
        out_shape=jax.ShapeDtypeStruct(matrix.shape, jnp.float32),
        scratch_shapes=[pltpu.VMEM(matrix.shape, jnp.float32)],
        compiler_params=pltpu.CompilerParams(vmem_limit_bytes=12 * megabyte),
        cost_estimate=pl.CostEstimate(flops=10**8, bytes_accessed=10**6, transcendentals=0),
        name="lower_inverse",
    )(matrix)


def aligned(depth, sizes):
    return depth % 128 == 0 and all(size % 128 == 0 for size in sizes)


def taken(activations, depth, rels, start, size):
    blocks = activations.reshape(activations.shape[0], -1, depth)[:, :, start : start + size]
    return jnp.take(blocks, jnp.asarray(rels, jnp.int32) ^ lax.axis_index("dp"), axis=1).transpose(1, 0, 2)


def chosen(activations, depth, rels, cuts):
    if not aligned(depth, [size for _, size in cuts]):
        return [taken(activations, depth, own, *part) for own, part in zip(rels, cuts)]
    own = activations.shape[0]
    here = lax.axis_index("dp")[None]

    def kernel(here_ref, in_ref, *refs):
        out_refs, sems = refs[:-1], refs[-1]
        copies = []
        for c, (start, size) in enumerate(cuts):
            for i, rel in enumerate(rels[c]):
                at = pl.multiple_of((here_ref[0] ^ rel) * depth + start, 128)
                source = in_ref.at[:, pl.ds(at, size)]
                copies.append(pltpu.make_async_copy(source, out_refs[c].at[i], sems.at[c, i]))
        for copy in copies:
            copy.start()
        for copy in copies:
            copy.wait()

    anywhere = pl.BlockSpec(memory_space=pl.ANY)
    return pl.pallas_call(
        kernel,
        in_specs=[pl.BlockSpec(memory_space=pltpu.SMEM), anywhere],
        out_specs=[pl.BlockSpec(memory_space=pltpu.VMEM)] * len(cuts),
        out_shape=[jax.ShapeDtypeStruct((len(rels[0]), own, size), activations.dtype) for _, size in cuts],
        scratch_shapes=[pltpu.SemaphoreType.DMA((len(cuts), len(rels[0])))],
        compiler_params=pltpu.CompilerParams(vmem_limit_bytes=56 * megabyte),
        cost_estimate=pl.CostEstimate(flops=0, bytes_accessed=6 * 10**6, transcendentals=0),
        name="chosen",
    )(here, activations)


def partials(left, activations, depth, rels, cuts, paired):
    rank = left.shape[0]
    if not aligned(depth, [size for _, size in cuts]):
        outs = []
        for own, part, pair in zip(rels, cuts, paired):
            rows = taken(activations, depth, own, *part)
            term = jnp.einsum("kt,rtb->rkb", left, rows, preferred_element_type=jnp.float32)
            if pair is not None:
                term = term + jnp.einsum("kt,rtb->rkb", pair[0], pair[1], preferred_element_type=jnp.float32)
            outs.append(term.astype(jnp.bfloat16))
        return outs
    source = jnp.asarray(rels, jnp.int32) ^ lax.axis_index("dp")
    pairs = [pair for pair in paired if pair is not None]

    def kernel(source_ref, left_ref, block_ref, *refs):
        others = list(refs[: 2 * len(pairs)])
        for c, ((start, size), pair) in enumerate(zip(cuts, paired)):
            out_ref = refs[2 * len(pairs) + c]
            other_left_ref, other_ref = (others.pop(0), others.pop(0)) if pair is not None else (None, None)

            def one(i, carry):
                at = pl.multiple_of(source_ref[c, i] * depth + start, 128)
                term = jnp.dot(left_ref[...], block_ref[:, pl.ds(at, size)], preferred_element_type=jnp.float32)
                if other_ref is not None:
                    term = term + jnp.dot(other_left_ref[...], other_ref[i], preferred_element_type=jnp.float32)
                out_ref[i] = term.astype(out_ref.dtype)
                return carry

            lax.fori_loop(0, len(rels[c]), one, 0)

    vmem = pl.BlockSpec(memory_space=pltpu.VMEM)
    return pl.pallas_call(
        kernel,
        in_specs=[pl.BlockSpec(memory_space=pltpu.SMEM)] + [vmem] * (2 + 2 * len(pairs)),
        out_specs=[vmem] * len(cuts),
        out_shape=[jax.ShapeDtypeStruct((len(rels[0]), rank, size), jnp.bfloat16) for _, size in cuts],
        compiler_params=pltpu.CompilerParams(vmem_limit_bytes=24 * megabyte),
        cost_estimate=pl.CostEstimate(flops=10**9, bytes_accessed=5 * 10**6, transcendentals=0),
        name="partials",
    )(source, left, activations, *[value for pair in pairs for value in pair])


def finish(kept, arrived, tokens):
    rank = kept[0].shape[1]
    sizes = [value.shape[2] for value in kept]
    depth = sum(sizes)
    if not aligned(depth, sizes):
        columns = [a[0].astype(jnp.float32) + b[0].astype(jnp.float32) for a, b in zip(kept, arrived)]
        columns = jnp.concatenate(columns, axis=1) / tokens
        return columns.astype(jnp.bfloat16).T, mul(columns, columns, ((1,), (1,)))

    def kernel(*refs):
        rows_ref, moment_ref = refs[-2:]
        start, moment = 0, 0.0
        for c, size in enumerate(sizes):
            columns = (refs[c][0].astype(jnp.float32) + refs[len(sizes) + c][0].astype(jnp.float32)) * (1.0 / tokens)
            moment = moment + mul(columns, columns, ((1,), (1,)))
            rows_ref[start : start + size, :] = columns.T.astype(rows_ref.dtype)
            start += size
        moment_ref[...] = moment

    return pl.pallas_call(
        kernel,
        out_shape=[
            jax.ShapeDtypeStruct((depth, rank), jnp.bfloat16),
            jax.ShapeDtypeStruct((rank, rank), jnp.float32),
        ],
        compiler_params=pltpu.CompilerParams(vmem_limit_bytes=10 * megabyte),
        cost_estimate=pl.CostEstimate(flops=10**9, bytes_accessed=3 * 10**6, transcendentals=0),
        name="finish",
    )(*kept, *arrived)


def project(me, gradient, total, factors, rels, starts, depth):
    rank, width = factors[0].shape[2], gradient.shape[1]

    tallest = max(value.shape[0] * value.shape[1] for value in factors)

    def kernel(me_ref, total_ref, gradient_ref, *refs):
        ins, (out_ref, held, facing, sems) = refs[: len(factors)], refs[len(factors) :]

        def fetch(q):
            size = factors[q].shape[1]
            out = []
            for b, rel in enumerate(rels[q]):
                at = pl.multiple_of((me_ref[0] ^ rel) * depth + starts[q], 16)
                rows = pl.ds(b * size, size)
                out.append(pltpu.make_async_copy(ins[q].at[b], held.at[q % 3, rows], sems.at[q % 3, 2 * b]))
                source = gradient_ref.at[pl.ds(at, size)]
                out.append(pltpu.make_async_copy(source, facing.at[q % 3, rows], sems.at[q % 3, 2 * b + 1]))
            return out

        for q in range(min(2, len(factors))):
            for copy in fetch(q):
                copy.start()
        out_ref[...] = total_ref[...]
        for q, factor in enumerate(factors):
            for copy in fetch(q):
                copy.wait()
            if q + 2 < len(factors):
                for copy in fetch(q + 2):
                    copy.start()
            rows = slice(0, factor.shape[0] * factor.shape[1])
            out_ref[...] += low_mul(held[q % 3, rows, :], facing[q % 3, rows, :], ((0,), (0,)))

    return pl.pallas_call(
        kernel,
        in_specs=[pl.BlockSpec(memory_space=pltpu.SMEM), pl.BlockSpec(memory_space=pltpu.VMEM)]
        + [pl.BlockSpec(memory_space=pl.ANY)] * (1 + len(factors)),
        out_specs=pl.BlockSpec(memory_space=pltpu.VMEM),
        out_shape=jax.ShapeDtypeStruct((rank, width), jnp.float32),
        scratch_shapes=[
            pltpu.VMEM((3, tallest, rank), factors[0].dtype),
            pltpu.VMEM((3, tallest, width), gradient.dtype),
            pltpu.SemaphoreType.DMA((3, 2 * max(len(own) for own in rels))),
        ],
        compiler_params=pltpu.CompilerParams(vmem_limit_bytes=28 * megabyte),
        cost_estimate=pl.CostEstimate(flops=10**8, bytes_accessed=10**6, transcendentals=0),
        name="project",
    )(me, total, gradient, *factors)


def correct(me, solver, projected, gradient, factors, rels, cuts, part_of, depth):
    rank, width = projected[0].shape
    blocks = gradient.shape[0] // depth
    tile = max(t for t in range(16, min(depth, 512) + 1, 16) if depth % t == 0)
    found = {(part_of[q], rel): (q, b) for q in range(len(factors)) for b, rel in enumerate(rels[q])}

    def kernel(me_ref, solver_ref, *refs):
        projected_refs, (gradient_ref, *refs) = refs[: len(projected)], refs[len(projected) :]
        ins, (out_ref, weights_ref, held, facing, done, in_sems, out_sems) = refs[: len(factors)], refs[len(factors) :]

        def base(i):
            return pl.multiple_of((me_ref[0] ^ i) * depth, 16)

        def fetch(i):
            whole = gradient_ref.at[pl.ds(base(i), depth)]
            out = [pltpu.make_async_copy(whole, facing.at[i % 3], in_sems.at[i % 3, len(cuts)])]
            for c, (start, size) in enumerate(cuts):
                q, b = found[c, i]
                into = held.at[i % 3, pl.ds(start, size)]
                out.append(pltpu.make_async_copy(ins[q].at[b], into, in_sems.at[i % 3, c]))
            return out

        def store(i):
            return pltpu.make_async_copy(done.at[i % 2], out_ref.at[pl.ds(base(i), depth)], out_sems.at[i % 2])

        for i in range(min(2, blocks)):
            for copy in fetch(i):
                copy.start()
        total = projected_refs[0][...]
        for ref in projected_refs[1:]:
            total = total + ref[...]
        weights_ref[...] = mul(solver_ref[...], total).astype(weights_ref.dtype)
        for i in range(blocks):
            for copy in fetch(i):
                copy.wait()
            if i + 2 < blocks:
                for copy in fetch(i + 2):
                    copy.start()
            if i >= 2:
                store(i - 2).wait()

            def one(t, carry):
                rows = pl.ds(pl.multiple_of(t * tile, 16), tile)
                term = jnp.dot(held[i % 3, rows, :], weights_ref[...], preferred_element_type=jnp.float32)
                done[i % 2, rows, :] = (facing[i % 3, rows, :].astype(jnp.float32) - term).astype(done.dtype)
                return carry

            lax.fori_loop(0, depth // tile, one, 0)
            store(i).start()
        for i in range(max(0, blocks - 2), blocks):
            store(i).wait()

    vmem = pl.BlockSpec(memory_space=pltpu.VMEM)
    return pl.pallas_call(
        kernel,
        in_specs=[pl.BlockSpec(memory_space=pltpu.SMEM)]
        + [vmem] * (1 + len(projected))
        + [pl.BlockSpec(memory_space=pl.ANY)] * (1 + len(factors)),
        out_specs=pl.BlockSpec(memory_space=pl.ANY),
        out_shape=jax.ShapeDtypeStruct(gradient.shape, gradient.dtype),
        scratch_shapes=[
            pltpu.VMEM((rank, width), jnp.bfloat16),
            pltpu.VMEM((3, depth, rank), jnp.bfloat16),
            pltpu.VMEM((3, depth, width), gradient.dtype),
            pltpu.VMEM((2, depth, width), gradient.dtype),
            pltpu.SemaphoreType.DMA((3, len(cuts) + 1)),
            pltpu.SemaphoreType.DMA((2,)),
        ],
        compiler_params=pltpu.CompilerParams(vmem_limit_bytes=32 * megabyte),
        cost_estimate=pl.CostEstimate(flops=7 * 10**9, bytes_accessed=70 * 10**6, transcendentals=0),
        name="correct",
    )(me, solver, *projected, gradient, *factors)


def cut(extent, shares):
    unit = extent // sum(shares)
    out, start = [], 0
    for i, share in enumerate(shares):
        size = unit * share if i + 1 < len(shares) else extent - start
        out.append((start, size))
        start += size
    return out


def split_pairs(values, groups=2):
    size = len(values) // groups
    return [list(values[i * size : (i + 1) * size]) for i in range(groups)]


def local(activations, test_matrix, gradient):
    count = lax.axis_size("dp")
    me = lax.axis_index("dp")
    own, hidden = activations.shape
    tokens = own * count
    probes = test_matrix.shape[1]
    rank = probes * count
    depth = hidden // count
    bx, by, bl = 1, 2, 4
    lead = [1 << i for i in range(3, count.bit_length() - 1)][::-1]
    every = list(range(count))
    rotations = ((bx, by, bl), (by, bl, bx), (bl, bx, by))

    parts = cut(depth, (4, 4, 3, 1, 1))
    orders = [
        lead + [bl, by],
        lead + [bx, bl],
        lead + [bl, by, bx],
        [by, bx] + lead + [bl],
        lead + [bl, bx, by],
    ]
    swaps = (bx, by)

    probe_rows = test_matrix.T
    give = chosen(activations, depth, [[r | bit for r in places(order)] for order, bit in zip(orders, swaps)], parts[:2])
    swapped = [across(value, bit) for value, bit in zip(give, swaps)]
    for bit in lead:
        probe_rows = jnp.concatenate([probe_rows, across(probe_rows, bit)], axis=0)
    probe_rows, *swapped = round_end(probe_rows, *swapped)
    strips = cut(hidden, (69, 69, 70))
    first = [probe_rows[:, start : start + size] for start, size in strips]
    arrived = [across(value, order[0]) for value, order in zip(first, rotations)]
    first = [jnp.concatenate(pair, axis=0) for pair in zip(first, arrived)]
    first = round_end(*first)
    second = [across(value, order[1]) for value, order in zip(first, rotations)]
    first, second = split_pairs(round_end(*first, *second))

    def sketch_of(strip, rows):
        start, size = strip
        return low_mul(activations[:, start : start + size], rows, ((1,), (1,)))

    third = [across(value, order[2]) for value, order in zip(first, rotations)]
    terms = [[sketch_of(strip, jnp.concatenate(pair, axis=0))] for strip, pair in zip(strips, zip(first, second))]
    ended = round_end(*third, *second, *[value for term in terms for value in term])
    third, second, terms = split_pairs(ended, 3)
    terms = [[value] for value in terms]
    fourth = [across(value, order[2]) for value, order in zip(second, rotations)]
    for term, strip, value in zip(terms, strips, third):
        term.append(sketch_of(strip, value))
    fourth = round_end(*fourth, *[value for term in terms for value in term])[: len(strips)]
    for term, strip, value in zip(terms, strips, fourth):
        term.append(sketch_of(strip, value))
    spread = []
    for order in rotations:
        source = jnp.asarray(places(lead + list(order)), jnp.int32) ^ me
        columns = jnp.repeat(source, probes) * probes + jnp.tile(jnp.arange(probes), count)
        spread.append((columns[:, None] == jnp.arange(rank)).astype(jnp.float32))
    terms = [value for term in terms for value in term]
    sketch = total_tensor(mul(jnp.concatenate(terms, axis=1), jnp.concatenate(spread, axis=0)))
    sketch_low = sketch.astype(jnp.bfloat16)
    left = sketch_low.T

    steps = [list(reversed(order)) for order in orders]
    rels = [places(order) for order in orders]
    half = [len(order) // 2 for order in rels]
    pairs = [None] * len(parts)
    sent, kept = [None] * len(parts), [None] * len(parts)
    for c in range(2, len(parts)):
        (sent[c],) = partials(left, activations, depth, [rels[c][half[c] :]], [parts[c]], [None])
    other_left = [across(left, bit) for bit in swaps]
    *other_left, sent[2] = round_end(*other_left, sent[2])
    for c in range(2):
        pair = (other_left[c], swapped[c])
        (sent[c],) = partials(
            left, activations, depth, [rels[c][half[c] :]], [parts[c]], [(pair[0], pair[1][half[c] :])]
        )
        pairs[c] = (pair[0], pair[1][: half[c]])
    left, sent[0], sent[1] = round_end(left, sent[0], sent[1])
    kept[2:] = partials(
        left, activations, depth, [rels[c][: half[c]] for c in range(2, len(parts))], parts[2:], pairs[2:]
    )
    kept[:2] = partials(left, activations, depth, [rels[c][: half[c]] for c in range(2)], parts[:2], pairs[:2])
    core = mul(sketch, sketch_low.astype(jnp.float32), ((0,), (0,)))
    core = my_half(core) if two_cores() else core
    turn = 0
    while True:
        arrived = [across(sent[c], step[0]) if step else None for c, step in enumerate(steps)]
        for bit in (lead, [], [bx, by], [bl], [])[min(turn, 4)]:
            core = core + across(core, bit)
        turn += 1
        for c, step in enumerate(steps):
            if len(step) > 1:
                cutting = kept[c].shape[0] // 2
                total = [
                    kept[c][rows].astype(jnp.float32) + arrived[c][rows].astype(jnp.float32)
                    for rows in (slice(cutting, None), slice(0, cutting))
                ]
                sent[c], kept[c] = [value.astype(jnp.bfloat16) for value in total]
                step.pop(0)
            elif step:
                sent[c] = arrived[c]
                step.pop(0)
        *ended, core = round_end(*sent, *kept, core)
        sent, kept = split_pairs(ended)
        if not any(steps):
            break
    rows, moment = finish(kept, sent, tokens)
    core = (both_halves(core) if two_cores() else core) / tokens
    core = 0.5 * (core + core.T)

    rows = rows[None]
    for bit in lead:
        rows = jnp.concatenate([rows, across(rows, bit)], axis=0)
    if two_cores():
        moment = my_half(moment) + other_core(my_half(moment, other=True))
    for bit in [bx, by, bl]:
        moment = moment + across(moment, bit)
    core, moment = round_end(core, moment)
    for bit in lead:
        moment = moment + across(moment, bit)
    inverse = lower_inverse(core)
    rows, inverse = round_end(rows, inverse)
    third = 16 * round(depth / 48)
    shares = [(0, third), (third, third), (2 * third, depth - 2 * third)]
    first = [rows[:, start : start + size] for start, size in shares]
    arrived = [across(value, order[0]) for value, order in zip(first, rotations)]
    moment = both_halves(moment) if two_cores() else lax.psum(moment, "tensor")
    first = [jnp.concatenate(pair, axis=0) for pair in zip(first, arrived)]
    first = round_end(*first)
    second = [across(value, order[1]) for value, order in zip(first, rotations)]
    gram = mul(mul(inverse, moment), inverse, ((1,), (1,)))
    damping = damping_ratio * jnp.trace(gram) / rank
    last = lower_inverse(gram + damping * jnp.eye(rank, dtype=jnp.float32))
    *both, gram, last = round_end(*first, *second, gram, last)
    first, second = split_pairs(both)
    starts = [start for start, _ in shares]
    near = [places(lead + [order[0]]) for order in rotations]
    next_to = [[r ^ order[1] for r in rs] for rs, order in zip(near, rotations)]
    far = [[r ^ order[2] for r in rs] for rs, order in zip(near, rotations)]
    farthest = [[r ^ order[2] for r in rs] for rs, order in zip(next_to, rotations)]
    here = me[None]
    third = [across(value, order[2]) for value, order in zip(first, rotations)]
    step = mul(last, inverse)
    solver = mul(step, step, ((0,), (0,)))
    projected = jnp.zeros((rank, gradient.shape[1]), jnp.float32)
    projected = project(here, gradient, projected, first + second, near + next_to, starts * 2, depth)
    *ended, solver, projected = round_end(*third, *second, solver, projected)
    third, second = split_pairs(ended)
    fourth = [across(value, order[2]) for value, order in zip(second, rotations)]
    projected = project(here, gradient, projected, third, far, starts, depth)
    *fourth, projected = round_end(*fourth, projected)
    projected = project(here, gradient, projected, fourth, farthest, starts, depth)
    projected = (projected, other_core(projected)) if two_cores() else (lax.psum(projected, "tensor"),)
    out = correct(
        here,
        solver,
        projected,
        gradient,
        first + second + third + fourth,
        near + next_to + far + farthest,
        shares,
        [0, 1, 2] * 4,
        depth,
    )
    return out, gram


def solution(mesh):
    placed = (P("dp", "tensor"), P("tensor", "dp"), P("tensor", "dp"))
    return jax.shard_map(
        local, mesh=mesh, in_specs=placed, out_specs=(P("tensor", "dp"), P()), check_vma=False
    )
```

```python
import jax
import jax.numpy as jnp
from jax import lax
from jax.experimental import pallas as pl
from jax.experimental.pallas import tpu as pltpu
from jax.sharding import PartitionSpec as P

damping_ratio = 0.1
exact = lax.Precision.HIGHEST
megabyte = 1024 * 1024


def mul(a, b, dims=((1,), (0,))):
    return lax.dot_general(a, b, (dims, ((), ())), precision=exact, preferred_element_type=jnp.float32)


def low_mul(a, b, dims=((1,), (0,))):
    return lax.dot_general(a, b, (dims, ((), ())), preferred_element_type=jnp.float32)


def across(value, bit):
    count = lax.axis_size("dp")
    return lax.ppermute(value, "dp", [(i, i ^ bit) for i in range(count)])


def total_tensor(value):
    return value + other_core(value) if two_cores() else lax.psum(value, "tensor")


def two_cores():
    return lax.axis_size("tensor") == 2


def my_half(value, other=False):
    half = value.shape[0] // 2
    core = lax.axis_index("tensor")
    return lax.dynamic_slice_in_dim(value, (1 - core if other else core) * half, half, axis=0)


def other_core(value):
    return lax.ppermute(value, "tensor", [(0, 1), (1, 0)])


def both_halves(mine):
    theirs = other_core(mine)
    first = lax.axis_index("tensor") == 0
    return jnp.concatenate([jnp.where(first, mine, theirs), jnp.where(first, theirs, mine)], axis=0)


def round_end(*values):
    return lax.optimization_barrier(values)


def places(bits):
    found = [0]
    for bit in bits:
        found = found + [i ^ bit for i in found]
    return found


def small_inverse(block):
    side = block.shape[0]
    lanes = lax.broadcasted_iota(jnp.int32, (side, side), 1)
    eye = (lax.broadcasted_iota(jnp.int32, (side, side), 0) == lanes).astype(jnp.float32)
    full = jnp.concatenate([block, eye], axis=1)
    work = [full[g : g + 8] for g in range(0, side, 8)]
    pivots = [jnp.ones((8, 1), jnp.float32) for _ in work]
    rows = lax.broadcasted_iota(jnp.int32, (8, 1), 0)
    for j in range(side):
        own, r = divmod(j, 8)
        row = work[own][r : r + 1, :]
        pivot = row[:, j : j + 1]
        pivots[own] = jnp.where(rows == r, pivot, pivots[own])
        unit = row * (1.0 / pivot)
        if r < 7:
            work[own] = work[own] - jnp.where(rows > r, work[own][:, j : j + 1], 0.0) * unit
        for g in range(own + 1, len(work)):
            work[g] = work[g] - work[g][:, j : j + 1] * unit
    return jnp.concatenate([w[:, side:] * lax.rsqrt(p) for w, p in zip(work, pivots)], axis=0)


def lower_inverse_kernel(matrix_ref, out_ref, left_ref):
    size = matrix_ref.shape[0]
    side = min(128, size)
    out_ref[...] = jnp.zeros(out_ref.shape, jnp.float32)
    left_ref[...] = matrix_ref[...]
    for k in range(0, size, side):
        own = pl.ds(k, side)
        block = small_inverse(left_ref[own, k : k + side])
        if k:
            out_ref[own, :k] = -mul(block, mul(left_ref[own, :k], out_ref[:k, :k]))
        out_ref[own, k : k + side] = block
        if k + side < size:
            rest = pl.ds(k + side, size - k - side)
            lower = mul(left_ref[rest, k : k + side], block, ((1,), (1,)))
            left_ref[rest, k : k + side] = lower
            left_ref[rest, k + side :] = left_ref[rest, k + side :] - mul(lower, lower, ((1,), (1,)))


def lower_inverse(matrix):
    return pl.pallas_call(
        lower_inverse_kernel,
        out_shape=jax.ShapeDtypeStruct(matrix.shape, jnp.float32),
        scratch_shapes=[pltpu.VMEM(matrix.shape, jnp.float32)],
        compiler_params=pltpu.CompilerParams(vmem_limit_bytes=12 * megabyte),
        cost_estimate=pl.CostEstimate(flops=10**8, bytes_accessed=10**6, transcendentals=0),
        name="lower_inverse",
    )(matrix)


def aligned(depth, sizes):
    return depth % 128 == 0 and all(size % 128 == 0 for size in sizes)


def taken(activations, depth, rels, start, size):
    blocks = activations.reshape(activations.shape[0], -1, depth)[:, :, start : start + size]
    return jnp.take(blocks, jnp.asarray(rels, jnp.int32) ^ lax.axis_index("dp"), axis=1).transpose(1, 0, 2)


def damped_kernel(moment_ref, inverse_ref, gram_ref, out_ref, shifted_ref, left_ref):
    gram = mul(mul(inverse_ref[...], moment_ref[...]), inverse_ref[...], ((1,), (1,)))
    gram_ref[...] = gram
    same = lax.broadcasted_iota(jnp.int32, gram.shape, 0) == lax.broadcasted_iota(jnp.int32, gram.shape, 1)
    trace = jnp.sum(jnp.where(same, gram, 0.0), keepdims=True)
    shifted_ref[...] = gram + jnp.where(same, damping_ratio * trace / gram.shape[0], 0.0)
    lower_inverse_kernel(shifted_ref, out_ref, left_ref)


def damped_inverse(moment, inverse):
    return pl.pallas_call(
        damped_kernel,
        out_shape=[jax.ShapeDtypeStruct(moment.shape, jnp.float32)] * 2,
        scratch_shapes=[pltpu.VMEM(moment.shape, jnp.float32)] * 2,
        compiler_params=pltpu.CompilerParams(vmem_limit_bytes=16 * megabyte),
        cost_estimate=pl.CostEstimate(flops=10**8, bytes_accessed=10**6, transcendentals=0),
        name="damped_inverse",
    )(moment, inverse)


def chosen(activations, depth, rels, cuts):
    if not aligned(depth, [size for _, size in cuts]):
        return [taken(activations, depth, own, *part) for own, part in zip(rels, cuts)]
    own = activations.shape[0]
    here = lax.axis_index("dp")[None]

    def kernel(here_ref, in_ref, *refs):
        out_refs, sems = refs[:-1], refs[-1]
        copies = []
        for c, (start, size) in enumerate(cuts):
            for i, rel in enumerate(rels[c]):
                at = pl.multiple_of((here_ref[0] ^ rel) * depth + start, 128)
                source = in_ref.at[:, pl.ds(at, size)]
                copies.append(pltpu.make_async_copy(source, out_refs[c].at[i], sems.at[c, i]))
        for copy in copies:
            copy.start()
        for copy in copies:
            copy.wait()

    anywhere = pl.BlockSpec(memory_space=pl.ANY)
    return pl.pallas_call(
        kernel,
        in_specs=[pl.BlockSpec(memory_space=pltpu.SMEM), anywhere],
        out_specs=[pl.BlockSpec(memory_space=pltpu.VMEM)] * len(cuts),
        out_shape=[jax.ShapeDtypeStruct((len(rels[0]), own, size), activations.dtype) for _, size in cuts],
        scratch_shapes=[pltpu.SemaphoreType.DMA((len(cuts), len(rels[0])))],
        compiler_params=pltpu.CompilerParams(vmem_limit_bytes=56 * megabyte),
        cost_estimate=pl.CostEstimate(flops=0, bytes_accessed=6 * 10**6, transcendentals=0),
        name="chosen",
    )(here, activations)


def partials(left, activations, depth, rels, cuts, paired):
    rank = left.shape[0]
    if not aligned(depth, [size for _, size in cuts]):
        outs = []
        for own, part, pair in zip(rels, cuts, paired):
            rows = taken(activations, depth, own, *part)
            term = jnp.einsum("kt,rtb->rkb", left, rows, preferred_element_type=jnp.float32)
            if pair is not None:
                term = term + jnp.einsum("kt,rtb->rkb", pair[0], pair[1], preferred_element_type=jnp.float32)
            outs.append(term.astype(jnp.bfloat16))
        return outs
    source = jnp.asarray(rels, jnp.int32) ^ lax.axis_index("dp")
    pairs = [pair for pair in paired if pair is not None]

    def kernel(source_ref, left_ref, block_ref, *refs):
        others = list(refs[: 2 * len(pairs)])
        for c, ((start, size), pair) in enumerate(zip(cuts, paired)):
            out_ref = refs[2 * len(pairs) + c]
            other_left_ref, other_ref = (others.pop(0), others.pop(0)) if pair is not None else (None, None)

            def one(i, carry):
                at = pl.multiple_of(source_ref[c, i] * depth + start, 128)
                term = jnp.dot(left_ref[...], block_ref[:, pl.ds(at, size)], preferred_element_type=jnp.float32)
                if other_ref is not None:
                    term = term + jnp.dot(other_left_ref[...], other_ref[i], preferred_element_type=jnp.float32)
                out_ref[i] = term.astype(out_ref.dtype)
                return carry

            lax.fori_loop(0, len(rels[c]), one, 0)

    vmem = pl.BlockSpec(memory_space=pltpu.VMEM)
    return pl.pallas_call(
        kernel,
        in_specs=[pl.BlockSpec(memory_space=pltpu.SMEM)] + [vmem] * (2 + 2 * len(pairs)),
        out_specs=[vmem] * len(cuts),
        out_shape=[jax.ShapeDtypeStruct((len(rels[0]), rank, size), jnp.bfloat16) for _, size in cuts],
        compiler_params=pltpu.CompilerParams(vmem_limit_bytes=24 * megabyte),
        cost_estimate=pl.CostEstimate(flops=10**9, bytes_accessed=5 * 10**6, transcendentals=0),
        name="partials",
    )(source, left, activations, *[value for pair in pairs for value in pair])


def finish(kept, arrived, tokens):
    rank = kept[0].shape[1]
    sizes = [value.shape[2] for value in kept]
    depth = sum(sizes)
    if not aligned(depth, sizes):
        columns = [a[0].astype(jnp.float32) + b[0].astype(jnp.float32) for a, b in zip(kept, arrived)]
        columns = jnp.concatenate(columns, axis=1) / tokens
        return columns.astype(jnp.bfloat16).T, mul(columns, columns, ((1,), (1,)))

    def kernel(*refs):
        rows_ref, moment_ref = refs[-2:]
        start, moment = 0, 0.0
        for c, size in enumerate(sizes):
            columns = (refs[c][0].astype(jnp.float32) + refs[len(sizes) + c][0].astype(jnp.float32)) * (1.0 / tokens)
            moment = moment + mul(columns, columns, ((1,), (1,)))
            rows_ref[start : start + size, :] = columns.T.astype(rows_ref.dtype)
            start += size
        moment_ref[...] = moment

    return pl.pallas_call(
        kernel,
        out_shape=[
            jax.ShapeDtypeStruct((depth, rank), jnp.bfloat16),
            jax.ShapeDtypeStruct((rank, rank), jnp.float32),
        ],
        compiler_params=pltpu.CompilerParams(vmem_limit_bytes=10 * megabyte),
        cost_estimate=pl.CostEstimate(flops=10**9, bytes_accessed=3 * 10**6, transcendentals=0),
        name="finish",
    )(*kept, *arrived)


def project(me, gradient, total, factors, rels, starts, depth):
    rank, width = factors[0].shape[2], gradient.shape[1]

    tallest = max(value.shape[0] * value.shape[1] for value in factors)

    def kernel(me_ref, total_ref, gradient_ref, *refs):
        ins, (out_ref, held, facing, sems) = refs[: len(factors)], refs[len(factors) :]

        def fetch(q):
            size = factors[q].shape[1]
            out = []
            for b, rel in enumerate(rels[q]):
                at = pl.multiple_of((me_ref[0] ^ rel) * depth + starts[q], 16)
                rows = pl.ds(b * size, size)
                out.append(pltpu.make_async_copy(ins[q].at[b], held.at[q % 3, rows], sems.at[q % 3, 2 * b]))
                source = gradient_ref.at[pl.ds(at, size)]
                out.append(pltpu.make_async_copy(source, facing.at[q % 3, rows], sems.at[q % 3, 2 * b + 1]))
            return out

        for q in range(min(2, len(factors))):
            for copy in fetch(q):
                copy.start()
        out_ref[...] = total_ref[...]
        for q, factor in enumerate(factors):
            for copy in fetch(q):
                copy.wait()
            if q + 2 < len(factors):
                for copy in fetch(q + 2):
                    copy.start()
            rows = slice(0, factor.shape[0] * factor.shape[1])
            out_ref[...] += low_mul(held[q % 3, rows, :], facing[q % 3, rows, :], ((0,), (0,)))

    return pl.pallas_call(
        kernel,
        in_specs=[pl.BlockSpec(memory_space=pltpu.SMEM), pl.BlockSpec(memory_space=pltpu.VMEM)]
        + [pl.BlockSpec(memory_space=pl.ANY)] * (1 + len(factors)),
        out_specs=pl.BlockSpec(memory_space=pltpu.VMEM),
        out_shape=jax.ShapeDtypeStruct((rank, width), jnp.float32),
        scratch_shapes=[
            pltpu.VMEM((3, tallest, rank), factors[0].dtype),
            pltpu.VMEM((3, tallest, width), gradient.dtype),
            pltpu.SemaphoreType.DMA((3, 2 * max(len(own) for own in rels))),
        ],
        compiler_params=pltpu.CompilerParams(vmem_limit_bytes=28 * megabyte),
        cost_estimate=pl.CostEstimate(flops=10**8, bytes_accessed=10**6, transcendentals=0),
        name="project",
    )(me, total, gradient, *factors)


def correct(me, solver, projected, gradient, factors, rels, cuts, part_of, depth):
    rank, width = projected[0].shape
    blocks = gradient.shape[0] // depth
    tile = max(t for t in range(16, min(depth, 512) + 1, 16) if depth % t == 0)
    found = {(part_of[q], rel): (q, b) for q in range(len(factors)) for b, rel in enumerate(rels[q])}

    def kernel(me_ref, solver_ref, *refs):
        projected_refs, (gradient_ref, *refs) = refs[: len(projected)], refs[len(projected) :]
        ins, (out_ref, weights_ref, held, facing, done, in_sems, out_sems) = refs[: len(factors)], refs[len(factors) :]

        def base(i):
            return pl.multiple_of((me_ref[0] ^ i) * depth, 16)

        def fetch(i):
            whole = gradient_ref.at[pl.ds(base(i), depth)]
            out = [pltpu.make_async_copy(whole, facing.at[i % 3], in_sems.at[i % 3, len(cuts)])]
            for c, (start, size) in enumerate(cuts):
                q, b = found[c, i]
                into = held.at[i % 3, pl.ds(start, size)]
                out.append(pltpu.make_async_copy(ins[q].at[b], into, in_sems.at[i % 3, c]))
            return out

        def store(i):
            return pltpu.make_async_copy(done.at[i % 2], out_ref.at[pl.ds(base(i), depth)], out_sems.at[i % 2])

        for i in range(min(2, blocks)):
            for copy in fetch(i):
                copy.start()
        total = projected_refs[0][...]
        for ref in projected_refs[1:]:
            total = total + ref[...]
        weights_ref[...] = mul(solver_ref[...], total).astype(weights_ref.dtype)
        for i in range(blocks):
            for copy in fetch(i):
                copy.wait()
            if i + 2 < blocks:
                for copy in fetch(i + 2):
                    copy.start()
            if i >= 2:
                store(i - 2).wait()

            def one(t, carry):
                rows = pl.ds(pl.multiple_of(t * tile, 16), tile)
                term = jnp.dot(held[i % 3, rows, :], weights_ref[...], preferred_element_type=jnp.float32)
                done[i % 2, rows, :] = (facing[i % 3, rows, :].astype(jnp.float32) - term).astype(done.dtype)
                return carry

            lax.fori_loop(0, depth // tile, one, 0)
            store(i).start()
        for i in range(max(0, blocks - 2), blocks):
            store(i).wait()

    vmem = pl.BlockSpec(memory_space=pltpu.VMEM)
    return pl.pallas_call(
        kernel,
        in_specs=[pl.BlockSpec(memory_space=pltpu.SMEM)]
        + [vmem] * (1 + len(projected))
        + [pl.BlockSpec(memory_space=pl.ANY)] * (1 + len(factors)),
        out_specs=pl.BlockSpec(memory_space=pl.ANY),
        out_shape=jax.ShapeDtypeStruct(gradient.shape, gradient.dtype),
        scratch_shapes=[
            pltpu.VMEM((rank, width), jnp.bfloat16),
            pltpu.VMEM((3, depth, rank), jnp.bfloat16),
            pltpu.VMEM((3, depth, width), gradient.dtype),
            pltpu.VMEM((2, depth, width), gradient.dtype),
            pltpu.SemaphoreType.DMA((3, len(cuts) + 1)),
            pltpu.SemaphoreType.DMA((2,)),
        ],
        compiler_params=pltpu.CompilerParams(vmem_limit_bytes=32 * megabyte),
        cost_estimate=pl.CostEstimate(flops=7 * 10**9, bytes_accessed=70 * 10**6, transcendentals=0),
        name="correct",
    )(me, solver, *projected, gradient, *factors)


def cut(extent, shares):
    unit = extent // sum(shares)
    out, start = [], 0
    for i, share in enumerate(shares):
        size = unit * share if i + 1 < len(shares) else extent - start
        out.append((start, size))
        start += size
    return out


def split_pairs(values, groups=2):
    size = len(values) // groups
    return [list(values[i * size : (i + 1) * size]) for i in range(groups)]


def local(activations, test_matrix, gradient):
    count = lax.axis_size("dp")
    me = lax.axis_index("dp")
    own, hidden = activations.shape
    tokens = own * count
    probes = test_matrix.shape[1]
    rank = probes * count
    depth = hidden // count
    bx, by, bl = 1, 2, 4
    lead = [1 << i for i in range(3, count.bit_length() - 1)][::-1]
    every = list(range(count))
    rotations = ((bx, by, bl), (by, bl, bx), (bl, bx, by))

    parts = cut(depth, (4, 4, 3, 1, 1))
    orders = [
        lead + [bl, by],
        lead + [bx, bl],
        lead + [bl, by, bx],
        [by, bx] + lead + [bl],
        lead + [bl, bx, by],
    ]
    swaps = (bx, by)

    probe_rows = test_matrix.T
    give = chosen(activations, depth, [[r | bit for r in places(order)] for order, bit in zip(orders, swaps)], parts[:2])
    swapped = [across(value, bit) for value, bit in zip(give, swaps)]
    for bit in lead:
        probe_rows = jnp.concatenate([probe_rows, across(probe_rows, bit)], axis=0)
    probe_rows, *swapped = round_end(probe_rows, *swapped)
    strips = cut(hidden, (69, 69, 70))
    first = [probe_rows[:, start : start + size] for start, size in strips]
    arrived = [across(value, order[0]) for value, order in zip(first, rotations)]
    first = [jnp.concatenate(pair, axis=0) for pair in zip(first, arrived)]
    first = round_end(*first)
    second = [across(value, order[1]) for value, order in zip(first, rotations)]
    first, second = split_pairs(round_end(*first, *second))

    def sketch_of(strip, rows):
        start, size = strip
        return low_mul(activations[:, start : start + size], rows, ((1,), (1,)))

    third = [across(value, order[2]) for value, order in zip(first, rotations)]
    terms = [[sketch_of(strip, jnp.concatenate(pair, axis=0))] for strip, pair in zip(strips, zip(first, second))]
    ended = round_end(*third, *second, *[value for term in terms for value in term])
    third, second, terms = split_pairs(ended, 3)
    terms = [[value] for value in terms]
    fourth = [across(value, order[2]) for value, order in zip(second, rotations)]
    for term, strip, value in zip(terms, strips, third):
        term.append(sketch_of(strip, value))
    fourth = round_end(*fourth, *[value for term in terms for value in term])[: len(strips)]
    for term, strip, value in zip(terms, strips, fourth):
        term.append(sketch_of(strip, value))
    spread = []
    for order in rotations:
        source = jnp.asarray(places(lead + list(order)), jnp.int32) ^ me
        columns = jnp.repeat(source, probes) * probes + jnp.tile(jnp.arange(probes), count)
        spread.append((columns[:, None] == jnp.arange(rank)).astype(jnp.float32))
    terms = [value for term in terms for value in term]
    sketch = total_tensor(mul(jnp.concatenate(terms, axis=1), jnp.concatenate(spread, axis=0)))
    sketch_low = sketch.astype(jnp.bfloat16)
    left = sketch_low.T

    steps = [list(reversed(order)) for order in orders]
    rels = [places(order) for order in orders]
    half = [len(order) // 2 for order in rels]
    pairs = [None] * len(parts)
    sent, kept = [None] * len(parts), [None] * len(parts)
    for c in range(2, len(parts)):
        (sent[c],) = partials(left, activations, depth, [rels[c][half[c] :]], [parts[c]], [None])
    other_left = [across(left, bit) for bit in swaps]
    *other_left, sent[2] = round_end(*other_left, sent[2])
    for c in range(2):
        pair = (other_left[c], swapped[c])
        (sent[c],) = partials(
            left, activations, depth, [rels[c][half[c] :]], [parts[c]], [(pair[0], pair[1][half[c] :])]
        )
        pairs[c] = (pair[0], pair[1][: half[c]])
    left, sent[0], sent[1] = round_end(left, sent[0], sent[1])
    kept[2:] = partials(
        left, activations, depth, [rels[c][: half[c]] for c in range(2, len(parts))], parts[2:], pairs[2:]
    )
    kept[:2] = partials(left, activations, depth, [rels[c][: half[c]] for c in range(2)], parts[:2], pairs[:2])
    core = mul(sketch, sketch_low.astype(jnp.float32), ((0,), (0,)))
    core = my_half(core) if two_cores() else core
    turn = 0
    while True:
        arrived = [across(sent[c], step[0]) if step else None for c, step in enumerate(steps)]
        for bit in (lead, [], [bx, by], [bl], [])[min(turn, 4)]:
            core = core + across(core, bit)
        turn += 1
        for c, step in enumerate(steps):
            if len(step) > 1:
                cutting = kept[c].shape[0] // 2
                total = [
                    kept[c][rows].astype(jnp.float32) + arrived[c][rows].astype(jnp.float32)
                    for rows in (slice(cutting, None), slice(0, cutting))
                ]
                sent[c], kept[c] = [value.astype(jnp.bfloat16) for value in total]
                step.pop(0)
            elif step:
                sent[c] = arrived[c]
                step.pop(0)
        *ended, core = round_end(*sent, *kept, core)
        sent, kept = split_pairs(ended)
        if not any(steps):
            break
    rows, moment = finish(kept, sent, tokens)
    core = (both_halves(core) if two_cores() else core) / tokens
    core = 0.5 * (core + core.T)

    rows = rows[None]
    for bit in lead:
        rows = jnp.concatenate([rows, across(rows, bit)], axis=0)
    if two_cores():
        moment = my_half(moment) + other_core(my_half(moment, other=True))
    for bit in [bx, by, bl]:
        moment = moment + across(moment, bit)
    inverse = lower_inverse(core)
    rows, moment, inverse = round_end(rows, moment, inverse)
    third = 16 * round(depth / 48)
    shares = [(0, third), (third, third), (2 * third, depth - 2 * third)]
    first = [rows[:, start : start + size] for start, size in shares]
    arrived = [across(value, order[0]) for value, order in zip(first, rotations)]
    for bit in lead:
        moment = moment + across(moment, bit)
    moment = both_halves(moment) if two_cores() else lax.psum(moment, "tensor")
    first = [jnp.concatenate(pair, axis=0) for pair in zip(first, arrived)]
    first = round_end(*first)
    second = [across(value, order[1]) for value, order in zip(first, rotations)]
    gram, last = damped_inverse(moment, inverse)
    *both, gram, last = round_end(*first, *second, gram, last)
    first, second = split_pairs(both)
    starts = [start for start, _ in shares]
    near = [places(lead + [order[0]]) for order in rotations]
    next_to = [[r ^ order[1] for r in rs] for rs, order in zip(near, rotations)]
    far = [[r ^ order[2] for r in rs] for rs, order in zip(near, rotations)]
    farthest = [[r ^ order[2] for r in rs] for rs, order in zip(next_to, rotations)]
    here = me[None]
    third = [across(value, order[2]) for value, order in zip(first, rotations)]
    step = mul(last, inverse)
    solver = mul(step, step, ((0,), (0,)))
    projected = jnp.zeros((rank, gradient.shape[1]), jnp.float32)
    projected = project(here, gradient, projected, first + second, near + next_to, starts * 2, depth)
    *ended, solver, projected = round_end(*third, *second, solver, projected)
    third, second = split_pairs(ended)
    fourth = [across(value, order[2]) for value, order in zip(second, rotations)]
    projected = project(here, gradient, projected, third, far, starts, depth)
    *fourth, projected = round_end(*fourth, projected)
    projected = project(here, gradient, projected, fourth, farthest, starts, depth)
    projected = (projected, other_core(projected)) if two_cores() else (lax.psum(projected, "tensor"),)
    out = correct(
        here,
        solver,
        projected,
        gradient,
        first + second + third + fourth,
        near + next_to + far + farthest,
        shares,
        [0, 1, 2] * 4,
        depth,
    )
    return out, gram


def solution(mesh):
    placed = (P("dp", "tensor"), P("tensor", "dp"), P("tensor", "dp"))
    return jax.shard_map(
        local, mesh=mesh, in_specs=placed, out_specs=(P("tensor", "dp"), P()), check_vma=False
    )
```
